256 devices in a mesh: section: 2 (over x_lo), tok: 64 (over y, z, core), head: 2 (over x_hi).
Axes of the slice: x: 4 (x_hi: 2, x_lo: 2; x = x_hi * 2 + x_lo), y: 4, z: 8, core: 2. Of those that a mesh axis runs over, the one named last changes fastest.
Arguments:
- queries: bfloat16 [2, 8192, 2048], P('section', 'tok', 'head'), may hold values from -6 to 6
- keyvals: bfloat16 [2, 8192, 2, 512], P('section', 'tok', None, 'head'), may hold values from -6 to 6
- span_req: int32 [2, 8192], P('section'), may hold values from 0 to 15, never falling along the last dimension, each value on 1 to 6144 neighbouring positions
- prefill_blocks: bfloat16 [3072, 2, 128, 512], P(('section', 'tok'), None, None, 'head'), may hold values from -6 to 6
- block_dest: int32 [3072], replicated, may hold values from 0 to 127, as said below
- out_weight: bfloat16 [2048, 2048], P('head'), may hold values from -0.125 to 0.125
Outputs:
- mixed: bfloat16 [2, 8192, 2048], P('section', 'tok', 'head')
- decode_blocks: bfloat16 [3072, 2, 128, 512], P(('section', 'tok'), None, None, 'head')
The draws below stay inside these ranges and needn't reach their ends.
Inputs may be any that keep to these rules, and one draw needn't show every extreme that they name: `span_req`: along each half's 8192 positions the request number never falls; one request covers exactly 6144 positions and none covers more. `block_dest`: blocks of one half of section go to shards of the other half; no shard receives two blocks from one source shard, and every shard receives exactly 24 blocks.
All inputs are finite; a program needn't handle non-finite values.
Results may differ from the reference program's by a relative error of at most 0.009.
Values may be sent and summed in bfloat16 or wider, within the bound.
A program may use at most 128 MiB of HBM per device.

```python
import math
import jax
import jax.numpy as jnp
import numpy as np
from jax import lax

D = 2048
HEADS = 32
KVH = 8
HD = 64
BLOCK = 128
SPAN = 8192
BLK_DEV = 24
NBLK = 3072
N_SECTION = 2
N_TOK = 64


def shared_fields(key):
    key_query = jax.random.fold_in(key, 101)
    key_keys = jax.random.fold_in(key, 202)
    key_vals = jax.random.fold_in(key, 303)
    query_vals = jnp.clip(1.6 * jax.random.normal(key_query, (N_SECTION, SPAN, HEADS, HD), jnp.float32), -6.0, 6.0)
    key_field = jnp.clip(1.6 * jax.random.normal(key_keys, (N_SECTION, SPAN, KVH, HD), jnp.float32), -6.0, 6.0)
    value_field = jnp.clip(jax.random.normal(key_vals, (N_SECTION, SPAN, KVH, HD), jnp.float32), -6.0, 6.0)
    return (query_vals, key_field, value_field)


def draw_queries(key, part):
    query_vals, key_field, value_field = shared_fields(key)
    return query_vals.reshape(N_SECTION, SPAN, HEADS * HD).astype(jnp.bfloat16)


def draw_keyvals(key, part):
    query_vals, key_field, value_field = shared_fields(key)
    stacked = jnp.stack([key_field.reshape(N_SECTION, SPAN, KVH * HD), value_field.reshape(N_SECTION, SPAN, KVH * HD)], axis=2)
    return stacked.astype(jnp.bfloat16)


def draw_block_dest(key, part):
    pieces = []
    for section_half in range(N_SECTION):
        half_key = jax.random.fold_in(key, 11 + section_half)
        key_shift, key_start, key_final, key_order = jax.random.split(half_key, 4)
        shifts = jax.random.permutation(key_shift, N_TOK)[:BLK_DEV]
        starting = jax.random.permutation(key_start, N_TOK)
        final_map = jax.random.permutation(key_final, N_TOK)

        def shuffled(order_key):
            return jax.random.permutation(order_key, BLK_DEV)
        orders = jax.vmap(shuffled)(jax.random.split(key_order, N_TOK))
        landing = (starting[:, None] + shifts[orders]) % N_TOK
        targets = final_map[landing] + (N_SECTION - 1 - section_half) * N_TOK
        pieces.append(targets.reshape(N_TOK * BLK_DEV))
    return jnp.concatenate(pieces, axis=0).astype(jnp.int32)


def steps_of(own_key, dims, shards, smallest, high):
    level, own = 1.0, jax.random.fold_in(own_key, 6)
    for axis_at, shards_of in shards:
        steps = jnp.exp(jax.random.uniform(jax.random.fold_in(own, axis_at), (shards_of,), jnp.float32, smallest / len(shards), high / len(shards)))
        level = level * jnp.repeat(steps, dims[axis_at] // shards_of).reshape([-1 if axis == axis_at else 1 for axis in range(len(dims))])
    return level


def length_profile(number_of, total, most, lean):
    weights = [(1 << 20) // math.isqrt(standing ** lean) + 1 for standing in range(2, number_of + 1)]
    spare, holding = total - most - (number_of - 1), [1] * (number_of - 1)
    while spare > 0:
        movable = [i for i in range(number_of - 1) if holding[i] < most]
        pool, budget = sum([weights[i] for i in movable]), spare
        for i in movable:
            extra = min(most - holding[i], max(1, budget * weights[i] // pool), spare)
            holding[i] = holding[i] + extra
            spare = spare - extra
    return np.array([most] + holding)


def ragged_sizes(stream_key, count, total, bound, slope):
    if count == 2:
        one = jax.random.randint(stream_key, (), max(1, total - bound), min(bound, total - 1) + 1)
        return jnp.stack([one, total - one])
    tallies = jnp.asarray(length_profile(count, total, bound, slope), jnp.int32)
    couples = (count - 1) // 2
    giver, receiver = tallies[1:1 + 2 * couples:2], tallies[2:2 + 2 * couples:2]
    slack = jnp.minimum(giver - 1, bound - receiver)
    passed = jax.random.randint(jax.random.fold_in(stream_key, 1), (couples,), 0, 1 << 20) % (slack + 1)
    tallies = tallies.at[1:1 + 2 * couples:2].set(giver - passed).at[2:2 + 2 * couples:2].set(receiver + passed)
    return tallies[jax.random.permutation(jax.random.fold_in(stream_key, 2), count)]


def gaussian(stream_key, extent, spread, limit, cuts=(), kind=jnp.bfloat16):
    result = jax.random.normal(stream_key, extent, jnp.float32) * spread
    if len(cuts) > 0:
        result = steps_of(stream_key, extent, cuts, -0.22, 0.18) * result
    return jnp.clip(result, min=-limit, max=limit).astype(kind)


def setup_inputs(seed: int = 0) -> dict:
    key_of = jax.random.split(jax.random.key(seed), 7)
    queries = draw_queries(jax.random.fold_in(key_of[6], 71), 0)
    keyvals = draw_keyvals(jax.random.fold_in(key_of[6], 71), 0)
    span_req = jax.vmap(lambda own: jnp.searchsorted(jnp.cumsum(ragged_sizes(own, max(2, N_TOK // 4), SPAN, 3 * SPAN // 4, 2)), jnp.arange(SPAN), side="right"))(jax.random.split(key_of[2], N_SECTION)).reshape((N_SECTION, SPAN)).astype(jnp.int32)
    prefill_blocks = gaussian(key_of[3], (NBLK, 2, BLOCK, KVH * HD), 1.0, 6.0, ((0, 128), (3, 2)))
    block_dest = draw_block_dest(jax.random.fold_in(key_of[6], 71), 0)
    out_weight = gaussian(key_of[5], (HEADS * HD, D), (HEADS * HD) ** -0.5, 0.125, ((0, 2),))
    return {"queries": queries, "keyvals": keyvals, "span_req": span_req, "prefill_blocks": prefill_blocks, "block_dest": block_dest, "out_weight": out_weight}


def attend_half(query_half, keyval_half, segment_half):
    keys_all = keyval_half[:, 0].astype(jnp.float32).reshape(SPAN, KVH, HD)
    vals_all = keyval_half[:, 1].astype(jnp.float32).reshape(SPAN, KVH, HD)
    row_block = min(SPAN, 128)
    block_count = SPAN // row_block
    grouped = query_half.reshape(block_count, row_block, KVH, HEADS // KVH, HD)
    first_rows = jnp.arange(block_count, dtype=jnp.int32) * row_block
    key_positions = jnp.arange(SPAN, dtype=jnp.int32)
    score_scale = 1.0 / (HD ** 0.5)

    def one_block(inputs):
        query_block, first_row = inputs
        query_rows = first_row + jnp.arange(row_block, dtype=jnp.int32)
        query_segs = lax.dynamic_slice_in_dim(segment_half, first_row, row_block)
        allowed = (query_segs[:, None] == segment_half[None, :]) & (key_positions[None, :] <= query_rows[:, None])
        scores = jnp.einsum("qcgd,kcd->qcgk", query_block.astype(jnp.float32), keys_all) * score_scale
        scores = jnp.where(allowed[:, None, None, :], scores, -jnp.inf)
        highest = jnp.max(scores, axis=-1)
        expo = jnp.exp(scores - highest[..., None])
        totals = jnp.sum(expo, axis=-1)
        weights = lax.optimization_barrier(expo.astype(jnp.bfloat16)).astype(jnp.float32)
        attended = jnp.einsum("qcgk,kcd->qcgd", weights, vals_all) / totals[..., None]
        return attended.reshape(row_block, HEADS * HD).astype(jnp.bfloat16)

    blocks = lax.map(one_block, (grouped, first_rows))
    return blocks.reshape(SPAN, HEADS * HD)


def reference(queries, keyvals, span_req, prefill_blocks, block_dest, out_weight):
    outputs = []
    for section_half in range(N_SECTION):
        attended = attend_half(queries[section_half], keyvals[section_half], span_req[section_half])
        mixed_half = jnp.dot(attended, out_weight, preferred_element_type=jnp.float32).astype(jnp.bfloat16)
        outputs.append(mixed_half)
    mixed = jnp.stack(outputs, axis=0)
    ordering = jnp.argsort(block_dest, stable=True).astype(jnp.int32)
    decode_blocks = jnp.take(prefill_blocks, ordering, axis=0)
    return mixed, decode_blocks
```

```python
import functools
import math

import jax
import jax.numpy as jnp
from jax import lax
from jax.experimental import pallas as pl
from jax.experimental.pallas import tpu as pltpu
from jax.sharding import Mesh
from jax.sharding import PartitionSpec as P

HEADS = 32
KVH = 8
HD = 64
NY, NZ, NC = 4, 8, 2
SHARDS = NY * NZ * NC
TOK = ("y", "z", "core")

Z_FIRST = (17, 13, 10, 4)
Y_SECOND = (18, 8)
Y_FIRST = (15, 7)
Z_SECOND = (20, 15, 11, 4)


def pack_rows(blocks, dest_list, shard_count):
    targets = jnp.arange(shard_count, dtype=jnp.int32)
    matches = dest_list[None, :] == targets[:, None]
    present = jnp.any(matches, axis=1)
    picked = jnp.argmax(matches, axis=1)
    chosen = jnp.take(blocks, picked, axis=0)
    return jnp.where(present[:, None, None, None], chosen, jnp.zeros_like(chosen))


def compact_rows(received, sender_table, receiver, per_shard):
    present = jnp.any(sender_table == receiver, axis=1)
    ranking = jnp.cumsum(present.astype(jnp.int32)) - 1
    slot_ids = jnp.arange(per_shard, dtype=jnp.int32)
    matches = (ranking[None, :] == slot_ids[:, None]) & present[None, :]
    picked = jnp.argmax(matches, axis=1)
    return jnp.take(received, picked, axis=0)


def hand_over_padded(prefill_blocks, block_dest):
    per_shard = prefill_blocks.shape[0]
    section = lax.axis_index("section")
    tok = (lax.axis_index("y") * NZ + lax.axis_index("z")) * NC + lax.axis_index("core")
    dest_table = block_dest.reshape(-1, SHARDS, per_shard)
    moved = lax.ppermute(prefill_blocks, "section", [(0, 1), (1, 0)])
    sender_table = lax.dynamic_index_in_dim(dest_table, 1 - section, 0, keepdims=False)
    dest_list = lax.dynamic_index_in_dim(sender_table, tok, 0, keepdims=False)
    sending = pack_rows(moved, dest_list % SHARDS, SHARDS)
    received = lax.all_to_all(sending, TOK, split_axis=0, concat_axis=0, tiled=True)
    return compact_rows(received, sender_table, section * SHARDS + tok, per_shard)


def forward_share(plus, minus, far, cap):
    return jnp.clip((far + minus - plus + 1) // 2, jnp.maximum(0, far - cap), jnp.minimum(far, cap))


def ring_lists(step, valid, ring, cap):
    half = ring // 2
    step = jnp.where(valid, step, 0)
    plus = jnp.sum((step > 0) & (step < half), axis=-1, keepdims=True)
    minus = jnp.sum(step > half, axis=-1, keepdims=True)
    far = step == half
    share = forward_share(plus, minus, jnp.sum(far, axis=-1, keepdims=True), cap)
    count = step.shape[-1]
    spot = jnp.arange(count, dtype=jnp.int32)
    before = spot[None, :] < spot[:, None]
    far_rank = jnp.sum(far[..., None, :] & before, axis=-1)
    ahead = ((step > 0) & (step < half)) | (far & (far_rank < share))
    back = (step > 0) & ~ahead
    reach = jnp.where(ahead, step, jnp.where(back, ring - step, 0))
    key = reach * 256 + (255 - spot)
    same = (ahead[..., None, :] & ahead[..., :, None]) | (back[..., None, :] & back[..., :, None])
    rank = jnp.sum(same & (key[..., None, :] > key[..., :, None]), axis=-1)
    return ahead, back, reach, rank.astype(jnp.int32)


def pool_spots(ahead, back, reach, rank, base, caps):
    spot = jnp.zeros_like(rank)
    at = base
    for chosen in (ahead, back):
        for k, cap in enumerate(caps):
            spot = jnp.where(chosen & (reach == k + 1), at + rank, spot)
            at += cap
    return spot


def list_rows(chosen, rank, spot, cap):
    slots = jnp.arange(cap, dtype=jnp.int32)
    hit = (chosen.reshape(1, -1)) & (rank.reshape(1, -1) == slots[:, None])
    return jnp.sum(jnp.where(hit, spot.reshape(1, -1), 0), axis=1)


def ring_send(pool, rows_ahead, rows_back, axis, ring, caps):
    up = [(i, (i + 1) % ring) for i in range(ring)]
    down = [(i, (i - 1) % ring) for i in range(ring)]
    ahead = jnp.take(pool, rows_ahead, axis=0, mode="clip")
    back = jnp.take(pool, rows_back, axis=0, mode="clip")
    got_ahead, got_back = [], []
    for cap in caps:
        ahead = lax.ppermute(ahead[:cap], axis, up)
        back = lax.ppermute(back[:cap], axis, down)
        got_ahead.append(ahead)
        got_back.append(back)
    return got_ahead + got_back


def route(blocks, table, first, second):
    per_shard = blocks.shape[0]
    core = lax.axis_index("core")
    dest = lax.dynamic_index_in_dim(table, core, 2, keepdims=False)
    other = lax.dynamic_index_in_dim(table, 1 - core, 2, keepdims=False)
    me_y, me_z = lax.axis_index("y"), lax.axis_index("z")
    me = (me_y * NZ + me_z) * NC + core
    dest_y, dest_z = dest // (NZ * NC), dest // NC % NZ
    if first[0] == "y":
        turn = lambda a: jnp.swapaxes(a, 0, 1)
        dest_1, dest_2, me_1, me_2 = turn(dest_y), turn(dest_z), me_y, me_z
    else:
        turn = lambda a: a
        dest_1, dest_2, me_1, me_2 = dest_z, dest_y, me_z, me_y
    axis_1, ring_1, caps_1 = first
    axis_2, ring_2, caps_2 = second
    at_1 = jnp.arange(ring_1, dtype=jnp.int32)[None, :, None]
    at_2 = jnp.arange(ring_2, dtype=jnp.int32)[:, None]

    lists_1 = ring_lists((dest_1 - at_1) % ring_1, jnp.ones_like(dest_1, bool), ring_1, caps_1[-1])
    own = [lax.dynamic_index_in_dim(lax.dynamic_index_in_dim(a, me_2, 0, keepdims=False), me_1, 0, keepdims=False) for a in lists_1]
    index = jnp.arange(per_shard, dtype=jnp.int32)
    rows_ahead = list_rows(own[0], own[3], index, caps_1[0])
    rows_back = list_rows(own[1], own[3], index, caps_1[0])
    spots_1 = pool_spots(*lists_1, per_shard, caps_1)
    spots_1 = jnp.where(lists_1[2] == 0, index, spots_1)

    here = (dest_1 == me_1).reshape(ring_2, -1)
    lists_2 = ring_lists((dest_2.reshape(ring_2, -1) - at_2) % ring_2, here, ring_2, caps_2[-1])
    mine = [lax.dynamic_index_in_dim(a, me_2, 0, keepdims=False) for a in lists_2]
    spots_1 = spots_1.reshape(ring_2, -1)
    my_spots = lax.dynamic_index_in_dim(spots_1, me_2, 0, keepdims=False)
    next_ahead = list_rows(mine[0], mine[3], my_spots, caps_2[0])
    next_back = list_rows(mine[1], mine[3], my_spots, caps_2[0])
    pool_1 = per_shard + 2 * sum(caps_1)
    spots_2 = pool_spots(*lists_2, pool_1, caps_2)
    spots_2 = jnp.where(at_2 == me_2, spots_1, spots_2)
    spots_2 = turn(spots_2.reshape(ring_2, ring_1, per_shard)).reshape(NY * NZ, per_shard)

    mine_of = dest.reshape(NY * NZ, per_shard) == me
    theirs_of = dest.reshape(NY * NZ, per_shard) == me - core + (1 - core)
    far_of = other.reshape(NY * NZ, per_shard) == me
    mine_in, theirs_in, far_in = (jnp.any(a, axis=1) for a in (mine_of, theirs_of, far_of))
    spot_mine = jnp.sum(jnp.where(mine_of, spots_2, 0), axis=1)
    spot_theirs = jnp.sum(jnp.where(theirs_of, spots_2, 0), axis=1)
    chips = jnp.arange(NY * NZ, dtype=jnp.int32)
    before = chips[None, :] < chips[:, None]
    theirs_rank = jnp.sum(theirs_in[None, :] & before, axis=1)
    far_rank = jnp.sum(far_in[None, :] & before, axis=1)
    mine_rank = jnp.sum(mine_in[None, :] & before, axis=1)
    core_rows = list_rows(theirs_in, theirs_rank, spot_theirs, per_shard)
    pool_2 = pool_1 + 2 * sum(caps_2)
    slot_mine = mine_rank + far_rank + jnp.where(core == 1, far_in, False)
    slot_far = mine_rank + far_rank + jnp.where(core == 0, mine_in, False)
    final = list_rows(mine_in, slot_mine, spot_mine, per_shard) + list_rows(
        far_in, slot_far, pool_2 + far_rank, per_shard
    )

    pool = jnp.concatenate([blocks] + ring_send(blocks, rows_ahead, rows_back, axis_1, ring_1, caps_1), axis=0)
    pool = jnp.concatenate([pool] + ring_send(pool, next_ahead, next_back, axis_2, ring_2, caps_2), axis=0)
    crossed = lax.ppermute(jnp.take(pool, core_rows, axis=0, mode="clip"), "core", [(0, 1), (1, 0)])
    pool = jnp.concatenate([pool, crossed], axis=0)
    return jnp.take(pool, final, axis=0, mode="clip")


def counts_fit(steps, groups, ring, caps):
    half = ring // 2
    number = [jnp.sum(groups & (steps == k), axis=-1) for k in range(ring)]
    plus = sum(number[1:half])
    minus = sum(number[half + 1 :])
    share = forward_share(plus, minus, number[half], caps[-1])
    fits = jnp.bool_(True)
    for k in range(1, half + 1):
        ahead = sum(number[k:half]) + share
        back = sum(number[half + 1 : ring - k + 1]) + number[half] - share
        fits &= jnp.all(ahead <= caps[k - 1]) & jnp.all(back <= caps[k - 1])
    return fits


def lists_fit(table):
    y = jnp.arange(NY, dtype=jnp.int32)[:, None, None, None]
    z = jnp.arange(NZ, dtype=jnp.int32)[:, None, None]
    dest_y, dest_z = table // (NZ * NC), table // NC % NZ
    steps_y, steps_z = (dest_y - y) % NY, (dest_z - z) % NZ
    fits = counts_fit(steps_z, jnp.bool_(True), NZ, Z_FIRST)
    fits &= counts_fit(steps_y, jnp.bool_(True), NY, Y_FIRST)

    def columns(a):
        return jnp.moveaxis(a, 2, 3).reshape(2, NY, NC, 1, -1)

    def rows(a):
        return jnp.moveaxis(a, 1, 3).reshape(2, NZ, NC, 1, -1)

    to_z = jnp.arange(NZ, dtype=jnp.int32)[:, None]
    to_y = jnp.arange(NY, dtype=jnp.int32)[:, None]
    fits &= counts_fit(columns(steps_y), columns(dest_z) == to_z, NY, Y_SECOND)
    fits &= counts_fit(rows(steps_z), rows(dest_y) == to_y, NZ, Z_SECOND)
    return fits


def hand_over(prefill_blocks, block_dest):
    per_shard = prefill_blocks.shape[0]
    section = lax.axis_index("section")
    tables = (block_dest % SHARDS).reshape(2, NY, NZ, NC, per_shard)
    table_here = lax.dynamic_index_in_dim(tables, section, 0, keepdims=False)
    table_far = lax.dynamic_index_in_dim(tables, 1 - section, 0, keepdims=False)
    swap = [(0, 1), (1, 0)]
    with jax.named_scope("values_route"):
        values = lax.ppermute(prefill_blocks[:, 1], "section", swap)
        values = route(values, table_far, ("y", NY, Y_FIRST), ("z", NZ, Z_SECOND))
    with jax.named_scope("keys_route"):
        keys = route(prefill_blocks[:, 0], table_here, ("z", NZ, Z_FIRST), ("y", NY, Y_SECOND))
        keys = lax.ppermute(keys, "section", swap)
    routed = jnp.stack([keys, values], axis=1)
    return lax.cond(
        lists_fit(tables),
        lambda done, blocks, dest: done,
        lambda done, blocks, dest: hand_over_padded(blocks, dest),
        routed,
        prefill_blocks,
        block_dest,
    )


UNIT = 1024
SLAB = UNIT // NC


def attend_kernel(bounds, queries, kv, limits, out, high, total, accum):
    low_unit, high_unit, last_start, first_query = bounds[0], bounds[1], bounds[2], bounds[3]
    local_kv = queries.shape[0]
    high[...] = jnp.full_like(high, -1e30)
    total[...] = jnp.zeros_like(total)
    accum[...] = jnp.zeros_like(accum)
    first_head = bounds[4]

    def slab(unit, core, masked):
        base = (core * (NY * NZ) * 128) + unit * SLAB
        rows = pl.ds(pl.multiple_of(base, SLAB), SLAB)
        keys = kv[rows, :256]
        vals = kv[rows, 256:].T
        if masked:
            row = lax.broadcasted_iota(jnp.int32, (SLAB, queries.shape[1]), 0)
            pos = unit * UNIT + core * 128 + (row // 128) * 256 + row % 128
            kept = (pos >= limits[0:1, :]) & (pos <= limits[1:2, :])
        for c in range(local_kv):
            scores = lax.dot_general(
                keys, queries[c], (((1,), (1,)), ((), ())), preferred_element_type=jnp.float32
            )
            if masked:
                scores = jnp.where(kept, scores, -1e30)
            before = high[c : c + 1, :]
            now = jnp.maximum(before, jnp.max(scores, axis=0, keepdims=True))
            expo = jnp.exp(scores - now)
            factor = jnp.exp(before - now)
            high[c : c + 1, :] = now
            total[c : c + 1, :] = total[c : c + 1, :] * factor + jnp.sum(expo, axis=0, keepdims=True)
            part = lax.dot_general(
                vals[c * HD : (c + 1) * HD], expo.astype(jnp.bfloat16),
                (((1,), (0,)), ((), ())), preferred_element_type=jnp.float32,
            )
            accum[c] = accum[c] * factor + part

    def one_unit(unit, carry):
        inside = (unit * UNIT >= last_start) & (unit * UNIT + UNIT - 1 <= first_query)
        for core in range(NC):

            @pl.when(inside)
            def _():
                slab(unit, core, False)

            @pl.when(jnp.logical_not(inside))
            def _():
                slab(unit, core, True)

        return carry

    lax.fori_loop(low_unit, high_unit + 1, one_unit, 0)
    for c in range(local_kv):
        out[c] = (accum[c] / total[c : c + 1, :]).astype(out.dtype)


def attend(queries, kv, bounds, limits):
    local_kv, rows, _ = queries.shape
    vmem = pl.BlockSpec(memory_space=pltpu.VMEM)
    return pl.pallas_call(
        attend_kernel,
        out_shape=jax.ShapeDtypeStruct((local_kv, HD, rows), jnp.bfloat16),
        in_specs=[pl.BlockSpec(memory_space=pltpu.SMEM), vmem, vmem, vmem],
        out_specs=vmem,
        scratch_shapes=[
            pltpu.VMEM((8, rows), jnp.float32),
            pltpu.VMEM((8, rows), jnp.float32),
            pltpu.VMEM((local_kv, HD, rows), jnp.float32),
        ],
        compiler_params=pltpu.CompilerParams(vmem_limit_bytes=40 * 1024 * 1024),
        cost_estimate=pl.CostEstimate(
            flops=4 * local_kv * rows * 6144 * 256, bytes_accessed=10 * 2**20, transcendentals=local_kv * rows * 6144
        ),
    )(bounds, queries, kv, limits)


def per_device(queries, keyvals, span_req, prefill_blocks, block_dest, out_weight):
    tok_rows = queries.shape[1]
    local_kv = keyvals.shape[3] // HD
    group = HEADS // KVH
    tok = (lax.axis_index("y") * NZ + lax.axis_index("z")) * NC + lax.axis_index("core")
    first_query = tok * tok_rows
    segments = span_req[0]

    kv = keyvals[0].reshape(tok_rows, 2 * local_kv * HD)
    kv = lax.all_gather(kv, "z", axis=0, tiled=True)
    kv = lax.all_gather(kv, "y", axis=0, tiled=True)
    kv = lax.all_gather(kv, "core", axis=0, tiled=True)

    decode_blocks = hand_over(prefill_blocks, block_dest)

    own_segments = lax.dynamic_slice_in_dim(segments, first_query, tok_rows)
    starts = jnp.sum(segments[None, :] < own_segments[:, None], axis=1).astype(jnp.int32)
    places = first_query + jnp.arange(tok_rows, dtype=jnp.int32)
    limits = jnp.stack([jnp.tile(starts, group), jnp.tile(places, group)])
    bounds = jnp.stack([
        starts[0] // UNIT, (first_query + tok_rows - 1) // UNIT, starts[tok_rows - 1], first_query, jnp.int32(0)
    ])
    scaled = queries[0].reshape(tok_rows, local_kv, group, HD) * jnp.bfloat16(1.0 / math.sqrt(HD))
    own = jnp.eye(local_kv, dtype=jnp.bfloat16)
    spread = jnp.einsum("qcgd,ce->cgqed", scaled, own).reshape(local_kv, group * tok_rows, local_kv * HD)
    attended = attend(spread, kv, bounds, limits)
    attended = attended.reshape(local_kv, HD, group, tok_rows).transpose(3, 0, 2, 1).reshape(tok_rows, -1)

    width = out_weight.shape[1] // 2
    head = lax.axis_index("head")
    partial_out = jnp.dot(attended, out_weight, preferred_element_type=jnp.float32)
    away = lax.dynamic_slice_in_dim(partial_out, (1 - head) * width, width, 1).astype(jnp.bfloat16)
    kept = lax.dynamic_slice_in_dim(partial_out, head * width, width, 1)
    mixed = (kept + lax.ppermute(away, "head", [(0, 1), (1, 0)]).astype(jnp.float32)).astype(jnp.bfloat16)
    return mixed[None], decode_blocks


def solution(mesh):
    fine = Mesh(mesh.devices.reshape(2, NY, NZ, NC, 2), ("section",) + TOK + ("head",))
    return jax.shard_map(
        per_device,
        mesh=fine,
        in_specs=(
            P("section", TOK, "head"),
            P("section", TOK, None, "head"),
            P("section", None),
            P(("section",) + TOK, None, None, "head"),
            P(),
            P("head", None),
        ),
        out_specs=(P("section", TOK, "head"), P(("section",) + TOK, None, None, "head")),
        check_vma=False,
    )
```

```python
import functools
import math

import jax
import jax.numpy as jnp
from jax import lax
from jax.experimental import pallas as pl
from jax.experimental.pallas import tpu as pltpu
from jax.sharding import Mesh
from jax.sharding import PartitionSpec as P

HEADS = 32
KVH = 8
HD = 64
NY, NZ, NC = 4, 8, 2
BLK_DEV = 24
LONGEST = 6144
SHARDS = NY * NZ * NC
TOK = ("y", "z", "core")

Z_FIRST = (17, 13, 10, 4)
Y_SECOND = (18, 8)
Y_FIRST = (15, 7)
Z_SECOND = (20, 15, 11, 4)


def pack_rows(blocks, dest_list, shard_count):
    targets = jnp.arange(shard_count, dtype=jnp.int32)
    matches = dest_list[None, :] == targets[:, None]
    present = jnp.any(matches, axis=1)
    picked = jnp.argmax(matches, axis=1)
    chosen = jnp.take(blocks, picked, axis=0)
    return jnp.where(present[:, None, None, None], chosen, jnp.zeros_like(chosen))


def compact_rows(received, sender_table, receiver, per_shard):
    present = jnp.any(sender_table == receiver, axis=1)
    ranking = jnp.cumsum(present.astype(jnp.int32)) - 1
    slot_ids = jnp.arange(per_shard, dtype=jnp.int32)
    matches = (ranking[None, :] == slot_ids[:, None]) & present[None, :]
    picked = jnp.argmax(matches, axis=1)
    return jnp.take(received, picked, axis=0)


def hand_over_padded(prefill_blocks, block_dest):
    per_shard = prefill_blocks.shape[0]
    section = lax.axis_index("section")
    tok = (lax.axis_index("y") * NZ + lax.axis_index("z")) * NC + lax.axis_index("core")
    dest_table = block_dest.reshape(-1, SHARDS, per_shard)
    moved = lax.ppermute(prefill_blocks, "section", [(0, 1), (1, 0)])
    sender_table = lax.dynamic_index_in_dim(dest_table, 1 - section, 0, keepdims=False)
    dest_list = lax.dynamic_index_in_dim(sender_table, tok, 0, keepdims=False)
    sending = pack_rows(moved, dest_list % SHARDS, SHARDS)
    received = lax.all_to_all(sending, TOK, split_axis=0, concat_axis=0, tiled=True)
    return compact_rows(received, sender_table, section * SHARDS + tok, per_shard)


LANES = 32
POOL = 256
KEYS_COL, VALS_COL = 0, 8


def count_dot(a, b):
    return jnp.dot(a.astype(jnp.bfloat16), b.astype(jnp.bfloat16), preferred_element_type=jnp.float32)


def forward_share(number, ring, cap):
    half = ring // 2
    plus, minus, far = sum(number[1:half]), sum(number[half + 1 :]), number[half]
    even = jnp.floor((far + minus - plus + 1.0) * 0.5)
    return jnp.clip(even, jnp.maximum(0.0, far - cap), jnp.minimum(far, cap * 1.0))


def ring_lists(step, valid, before_of, total_of, ring, caps):
    half = ring // 2
    hot = [None] + [jnp.where(valid & (step == k), 1.0, 0.0) for k in range(1, ring)]
    tall = jnp.concatenate(hot[1:], axis=0)
    rows = step.shape[0]
    parts = lambda a: [None] + [a[k * rows : (k + 1) * rows] for k in range(ring - 1)]
    before, total = parts(count_dot(tall, before_of)), parts(count_dot(tall, total_of))
    number = [0.0] + total[1:]
    share = forward_share(number, ring, caps[-1])
    ahead_mask, back_mask = jnp.zeros_like(share), jnp.zeros_like(share)
    rank, spot = jnp.zeros_like(share), jnp.zeros_like(share)
    ahead_at = [sum(caps[:k]) for k in range(half)]
    back_at = [sum(caps) + at for at in ahead_at]
    far_ahead = hot[half] * jnp.where(before[half] < share, 1.0, 0.0)
    far_back = hot[half] - far_ahead
    for mask, place, at in (
        (far_ahead, before[half], ahead_at[half - 1]),
        (far_back, before[half] - share, back_at[half - 1]),
    ):
        rank += mask * place
        spot += mask * (place + at)
    ahead_mask += far_ahead
    back_mask += far_back
    for k in range(1, half):
        place = sum(number[k + 1 : half]) + share + before[k]
        rank += hot[k] * place
        spot += hot[k] * (place + ahead_at[k - 1])
        ahead_mask += hot[k]
        place = sum(number[half + 1 : ring - k]) + number[half] - share + before[ring - k]
        rank += hot[ring - k] * place
        spot += hot[ring - k] * (place + back_at[k - 1])
        back_mask += hot[ring - k]
    return ahead_mask, back_mask, rank, spot


def list_column(mask, rank, spot):
    slot = jnp.sum(mask * (rank + 1.0), axis=0, keepdims=True)
    code = jnp.sum(mask * spot, axis=0, keepdims=True)
    want = lax.broadcasted_iota(jnp.int32, (32, 1), 0).astype(jnp.float32) + 1.0
    return jnp.sum(jnp.where(slot == want, code, 0.0), axis=1, keepdims=True)


def wide_column(mask, rank, spot):
    want = lax.broadcasted_iota(jnp.int32, (32, 1), 0).astype(jnp.float32) + 1.0
    slot, code = mask * (rank + 1.0), mask * spot
    total = jnp.zeros((32, 1), jnp.float32)
    for row in range(mask.shape[0]):
        hit = slot[row : row + 1, :] == want
        total += jnp.sum(jnp.where(hit, code[row : row + 1, :], 0.0), axis=1, keepdims=True)
    return total


def route_plan(dest, other, y_first, me_y, me_z, core):
    rows, lanes = dest.shape
    ring_1, caps_1, ring_2, caps_2 = (NY, Y_FIRST, NZ, Z_SECOND) if y_first else (NZ, Z_FIRST, NY, Y_SECOND)
    me_1, me_2 = (me_y, me_z) if y_first else (me_z, me_y)
    lane = lax.broadcasted_iota(jnp.int32, (rows, lanes), 1)
    row = lax.broadcasted_iota(jnp.int32, (rows, lanes), 0)
    at_1, index = lane // LANES, (lane % LANES).astype(jnp.float32)
    valid = dest >= 0
    dest_y, dest_z = dest // (NZ * NC), dest // NC % NZ
    dest_1, dest_2 = (dest_y, dest_z) if y_first else (dest_z, dest_y)
    left = lax.broadcasted_iota(jnp.int32, (lanes, lanes), 0)
    right = lax.broadcasted_iota(jnp.int32, (lanes, lanes), 1)
    same = left // LANES == right // LANES
    one = lambda a: jnp.where(a, 1.0, 0.0)
    earlier = one(left < right)
    same_earlier, same_all = one(same & (left < right)), one(same)
    group_earlier = one(left // LANES < right // LANES)

    ahead, back, rank, spot = ring_lists(
        (dest_1 - at_1) & (ring_1 - 1), valid, same_earlier, same_all, ring_1, caps_1
    )
    own = one((row == me_2) & (at_1 == me_1))
    columns = [list_column(ahead * own, rank, index), list_column(back * own, rank, index)]
    moved = ahead + back
    spot_1 = jnp.where(moved > 0.5, POOL + spot, index)

    ahead, back, rank, spot = ring_lists(
        (dest_2 - row) & (ring_2 - 1), valid & (dest_1 == me_1), earlier, jnp.ones_like(earlier), ring_2, caps_2
    )
    own = one(row == me_2)
    columns += [list_column(ahead * own, rank, spot_1), list_column(back * own, rank, spot_1)]
    moved = ahead + back
    spot_2 = jnp.where(moved > 0.5, 2 * POOL + spot, spot_1)

    me = (me_y * NZ + me_z) * NC + core
    mine, theirs, far = one(dest == me), one(dest == me + 1 - 2 * core), one(other == me)

    def earlier_chips(hot):
        per_chip = count_dot(hot, same_all)
        if not y_first:
            below = jnp.zeros_like(hot)
            line = jnp.sum(hot, axis=1, keepdims=True)
            for r in range(rows):
                below += jnp.where(row > r, line[r : r + 1, :], 0.0)
            return below + count_dot(hot, group_earlier), per_chip
        below = jnp.zeros_like(hot)
        for r in range(rows):
            below += jnp.where(row > r, per_chip[r : r + 1, :], 0.0)
        whole = jnp.sum(hot, axis=0, keepdims=True)
        return below + count_dot(jnp.broadcast_to(whole, hot.shape), group_earlier), per_chip

    mine_at, mine_in = earlier_chips(mine)
    theirs_at, _ = earlier_chips(theirs)
    far_at, far_in = earlier_chips(far)
    second = core.astype(jnp.float32)
    columns.append(wide_column(theirs, theirs_at, spot_2))
    columns.append(
        wide_column(mine, mine_at + far_at + second * far_in, spot_2)
        + wide_column(far, mine_at + far_at + (1.0 - second) * mine_in, 3 * POOL + far_at)
    )
    return columns


def over_room(number, ring, caps):
    half = ring // 2
    share = forward_share(number, ring, caps[-1])
    worst = jnp.full_like(share, -1.0)
    for k in range(1, half + 1):
        ahead = sum(number[k:half]) + share
        back = sum(number[half + 1 : ring - k + 1]) + number[half] - share
        worst = jnp.maximum(worst, jnp.maximum(ahead, back) - caps[k - 1])
    return worst


def list_room(dest, y_first):
    rows, lanes = dest.shape
    ring_1, caps_1, ring_2, caps_2 = (NY, Y_FIRST, NZ, Z_SECOND) if y_first else (NZ, Z_FIRST, NY, Y_SECOND)
    lane = lax.broadcasted_iota(jnp.int32, (rows, lanes), 1)
    row = lax.broadcasted_iota(jnp.int32, (rows, lanes), 0)
    valid = dest >= 0
    dest_y, dest_z = dest // (NZ * NC), dest // NC % NZ
    dest_1, dest_2 = (dest_y, dest_z) if y_first else (dest_z, dest_y)
    step_1 = (dest_1 - lane // LANES) & (ring_1 - 1)
    step_2 = (dest_2 - row) & (ring_2 - 1)
    left = lax.broadcasted_iota(jnp.int32, (lanes, lanes), 0)
    right = lax.broadcasted_iota(jnp.int32, (lanes, lanes), 1)
    same = jnp.where(left // LANES == right // LANES, 1.0, 0.0)
    tall = jnp.concatenate([jnp.where(valid & (step_1 == k), 1.0, 0.0) for k in range(1, ring_1)], axis=0)
    tall = count_dot(tall, same)
    number = [0.0] + [tall[k * rows : (k + 1) * rows] for k in range(ring_1 - 1)]
    worst = jnp.max(over_room(number, ring_1, caps_1))
    for to in range(ring_1):
        here = valid & (dest_1 == to)
        number = [0.0] + [
            jnp.sum(jnp.where(here & (step_2 == k), 1.0, 0.0), axis=1, keepdims=True) for k in range(1, ring_2)
        ]
        worst = jnp.maximum(worst, jnp.max(over_room(number, ring_2, caps_2)))
    return worst


def plan_kernel(by_y, by_z, picks, room):
    section, core = lax.axis_index("section"), lax.axis_index("core")
    me_y, me_z = lax.axis_index("y"), lax.axis_index("z")
    keys = route_plan(by_y[section, core], by_y[section, 1 - core], False, me_y, me_z, core)
    vals = route_plan(by_z[1 - section, core], by_z[1 - section, 1 - core], True, me_y, me_z, core)
    lane = lax.broadcasted_iota(jnp.int32, (32, 128), 1)
    table = jnp.zeros((32, 128), jnp.float32)
    for base, columns in ((KEYS_COL, keys), (VALS_COL, vals)):
        for at, column in enumerate(columns):
            table = jnp.where(lane == base + at, column, table)
    picks[...] = table.astype(jnp.int32)
    worst = jnp.float32(-1.0)
    for half in range(2):
        for c in range(NC):
            worst = jnp.maximum(worst, list_room(by_y[half, c], False))
            worst = jnp.maximum(worst, list_room(by_z[half, c], True))
    room[...] = jnp.full(room.shape, worst, jnp.float32)


def plan_tables(block_dest):
    tables = (block_dest % SHARDS).reshape(2, NY, NZ, NC, BLK_DEV)
    tables = jnp.pad(tables, ((0, 0),) * 4 + ((0, LANES - BLK_DEV),), constant_values=-1)
    by_y = jnp.pad(
        tables.transpose(0, 3, 1, 2, 4).reshape(2, NC, NY, NZ * LANES),
        ((0, 0), (0, 0), (0, 8 - NY), (0, 0)), constant_values=-1,
    )
    by_z = tables.transpose(0, 3, 2, 1, 4).reshape(2, NC, NZ, NY * LANES)
    return by_y, by_z


def plan(block_dest):
    vmem = pl.BlockSpec(memory_space=pltpu.VMEM)
    return pl.pallas_call(
        plan_kernel,
        out_shape=(jax.ShapeDtypeStruct((32, 128), jnp.int32), jax.ShapeDtypeStruct((8, 128), jnp.float32)),
        in_specs=[vmem, vmem],
        out_specs=(vmem, vmem),
    )(*plan_tables(block_dest))


UNIT = 1024
SLAB = UNIT // NC
TOK_ROWS = 128
N_COPIES = 48


def pick(dst, count, picks, column, pools):
    def one(j, carry):
        code = picks[j, column]
        block = None
        for at, pool in enumerate(pools):
            if pool is None:
                continue
            row = jnp.clip(code - at * POOL, 0, pool.shape[0] - 1)
            found = pool[row]
            block = found if block is None else jnp.where(code >= at * POOL, found, block)
        dst[j] = block
        return carry

    lax.fori_loop(0, count, one, 0)


def move_kernel(
    picks, spread, kv_own, limits, weight, blocks, mixed, decoded,
    kv, w, keys_in, vals_in, vals_0, keys_st, keys_1, keys_2, keys_3, keys_end, vals_st, vals_1, vals_2, vals_3,
    high, total, accum, att, kept_out, away, got, local_sem, send_sem, recv_sem,
):
    section, core, head = lax.axis_index("section"), lax.axis_index("core"), lax.axis_index("head")
    y, z = lax.axis_index("y"), lax.axis_index("z")
    peers = {
        "x": {"section": 1 - section}, "core": {"core": 1 - core}, "head": {"head": 1 - head},
        "y+": {"y": (y + 1) % NY}, "y-": {"y": (y + NY - 1) % NY},
        "z+": {"z": (z + 1) % NZ}, "z-": {"z": (z + NZ - 1) % NZ},
    }
    count = [0]
    sends = []

    def send(src, dst, to):
        at = count[0]
        count[0] += 1
        copy = pltpu.make_async_remote_copy(
            src_ref=src, dst_ref=dst, send_sem=send_sem.at[at], recv_sem=recv_sem.at[at],
            device_id=peers[to], device_id_type=pl.DeviceIdType.MESH,
        )
        copy.start()
        sends.append(copy)
        return copy

    def sent(copies):
        for copy in copies:
            copy.wait_send()
            sends[:] = [c for c in sends if c is not copy]

    loads = [
        pltpu.make_async_copy(src, dst, local_sem.at[at])
        for at, (src, dst) in enumerate((
            (blocks.at[:, 1], vals_in), (kv_own, kv.at[(core * NY + y) * NZ + z]), (blocks.at[:, 0], keys_in), (weight, w),
        ))
    ]
    for load in loads:
        load.start()
    barrier = pltpu.get_barrier_semaphore()
    for peer in peers.values():
        pl.semaphore_signal(barrier, inc=1, device_id=peer, device_id_type=pl.DeviceIdType.MESH)
    pl.semaphore_wait(barrier, len(peers))

    def first_hops(stage, arrivals, axis, caps):
        cap, back = caps[0], sum(caps)
        return [
            send(stage.at[pl.ds(0, cap)], arrivals.at[pl.ds(0, cap)], axis + "+"),
            send(stage.at[pl.ds(cap, cap)], arrivals.at[pl.ds(back, cap)], axis + "-"),
        ]

    def next_hops(before, arrivals, axis, caps, k):
        came, at, back = sum(caps[: k - 1]), sum(caps[:k]), sum(caps)
        hops = []
        for copy, base, to in ((before[0], 0, "+"), (before[1], back, "-")):
            copy.wait_recv()
            hops.append(send(
                arrivals.at[pl.ds(base + came, caps[k])], arrivals.at[pl.ds(base + at, caps[k])], axis + to
            ))
        return hops

    def arrived(hops):
        for copy in hops:
            copy.wait_recv()

    def pick_lists(stage, caps, column, pools):
        pick(stage.at[pl.ds(0, caps[0])], caps[0], picks, column, pools)
        pick(stage.at[pl.ds(caps[0], caps[0])], caps[0], picks, column + 1, pools)

    def shard_at(c, yy, zz):
        return (c * NY + yy) * NZ + zz

    loads[1].wait()
    own = kv.at[shard_at(core, y, z)]
    kv_hops = [send(own, own, "z+"), send(own, own, "z-")]
    loads[0].wait()
    swap_vals = send(vals_in, vals_0, "x")
    loads[2].wait()
    pick_lists(keys_st, Z_FIRST, KEYS_COL, [keys_in])
    keys_from = keys_z = first_hops(keys_st, keys_1, "z", Z_FIRST)

    for k in range(1, NZ // 2):
        kv_hops[0].wait_recv()
        kv_hops[1].wait_recv()
        ahead = kv.at[shard_at(core, y, (z - k + NZ) % NZ)]
        back = kv.at[shard_at(core, y, (z + k) % NZ)]
        kv_hops[0] = send(ahead, ahead, "z+")
        if k < NZ // 2 - 1:
            kv_hops[1] = send(back, back, "z-")
    kv_hops[0].wait_recv()

    def line(yy):
        return kv.at[pl.ds(shard_at(core, yy, 0), NZ)]

    def part(yy, first):
        return kv.at[pl.ds(shard_at(core, yy, first), NZ // 2)]

    over, under = (y + 1) % NY, (y + NY - 1) % NY
    kv_y = [send(line(y), line(y), "y+"), send(line(y), line(y), "y-")]
    kv_core = [send(line(y), line(y), "core")]
    high[...] = jnp.full_like(high, -1e30)
    total[...] = jnp.zeros_like(total)
    accum[...] = jnp.zeros_like(accum)
    keys_z = next_hops(keys_z, keys_1, "z", Z_FIRST, 1)
    kv_y[0].wait_recv()
    kv_far = [send(part(under, 0), part(under, 0), "y+")]
    kv_core.append(send(line(under), line(under), "core"))
    kv_y[1].wait_recv()
    kv_far.append(send(part(over, NZ // 2), part(over, NZ // 2), "y-"))
    kv_core.append(send(line(over), line(over), "core"))
    swap_vals.wait_recv()
    pick_lists(vals_st, Y_FIRST, VALS_COL, [vals_0])
    vals_from = vals_y = first_hops(vals_st, vals_1, "y", Y_FIRST)
    keys_z = next_hops(keys_z, keys_1, "z", Z_FIRST, 2)
    arrived(kv_far)
    kv_core.append(send(line((y + 2) % NY), line((y + 2) % NY), "core"))
    arrived(kv_core)

    first_query = ((y * NZ + z) * NC + core) * TOK_ROWS
    local_kv, rows, _ = spread.shape

    def slab(half):
        unit, of_core = half // NC, half % NC
        at = shard_at(of_core, 0, 0) + unit * (SLAB // TOK_ROWS)
        block = kv[pl.ds(at, SLAB // TOK_ROWS)].reshape(SLAB, kv.shape[2])
        keys, vals = block[:, : local_kv * HD], block[:, local_kv * HD :].T
        row = lax.broadcasted_iota(jnp.int32, (SLAB, rows), 0)
        pos = unit * UNIT + of_core * TOK_ROWS + (row // TOK_ROWS) * (NC * TOK_ROWS) + row % TOK_ROWS
        keep = (pos >= limits[0:1, :]) & (pos <= limits[1:2, :])
        for c in range(local_kv):
            scores = lax.dot_general(
                keys, spread[c], (((1,), (1,)), ((), ())), preferred_element_type=jnp.float32
            )
            scores = jnp.where(keep, scores, -1e30)
            before = high[c : c + 1, :]
            now = jnp.maximum(before, jnp.max(scores, axis=0, keepdims=True))
            expo = jnp.exp(scores - now)
            factor = jnp.exp(before - now)
            high[c : c + 1, :] = now
            total[c : c + 1, :] = total[c : c + 1, :] * factor + jnp.sum(expo, axis=0, keepdims=True)
            accum[c] = accum[c] * factor + jnp.dot(
                vals[c * HD : (c + 1) * HD], expo.astype(jnp.bfloat16), preferred_element_type=jnp.float32
            )

    def units(low, top):
        def one(half, carry):
            start = half // NC * UNIT

            @pl.when((start < first_query + TOK_ROWS) & (start + UNIT > first_query - (LONGEST - 1)))
            def _():
                slab(half)

            return carry

        lax.fori_loop(low * NC, top * NC, one, 0)

    units(0, 2)
    keys_z = next_hops(keys_z, keys_1, "z", Z_FIRST, 3)
    vals_y = next_hops(vals_y, vals_1, "y", Y_FIRST, 1)
    arrived(keys_z)
    sent(keys_from)
    pick_lists(keys_st, Y_SECOND, KEYS_COL + 2, [keys_in, keys_1])
    keys_from = keys_y = first_hops(keys_st, keys_2, "y", Y_SECOND)
    arrived(vals_y)
    sent(vals_from)
    pick_lists(vals_st, Z_SECOND, VALS_COL + 2, [vals_0, vals_1])
    vals_from = vals_z = first_hops(vals_st, vals_2, "z", Z_SECOND)
    units(2, 6)
    keys_y = next_hops(keys_y, keys_2, "y", Y_SECOND, 1)
    vals_z = next_hops(vals_z, vals_2, "z", Z_SECOND, 1)
    arrived(keys_y)
    sent(keys_from)

    def between_cores(stage, arrivals, column, pools):
        pick(stage.at[pl.ds(0, BLK_DEV)], BLK_DEV, picks, column, pools)
        return send(stage.at[pl.ds(0, BLK_DEV)], arrivals, "core")

    keys_pools = [keys_in, keys_1, keys_2, keys_3]
    vals_pools = [vals_0, vals_1, vals_2, vals_3]
    crossing = between_cores(keys_st, keys_3, KEYS_COL + 4, keys_pools[:3])
    crossing.wait_recv()
    sent([crossing])
    pick(keys_st.at[pl.ds(0, BLK_DEV)], BLK_DEV, picks, KEYS_COL + 5, keys_pools)
    swap_keys = send(keys_st.at[pl.ds(0, BLK_DEV)], keys_end, "x")
    units(6, 8)
    vals_z = next_hops(vals_z, vals_2, "z", Z_SECOND, 2)

    group = rows // TOK_ROWS
    for c in range(local_kv):
        done = (accum[c] / total[c : c + 1, :]).astype(jnp.bfloat16)
        for g in range(group):
            at = (c * group + g) * HD
            att[at : at + HD, :] = done[:, g * TOK_ROWS : (g + 1) * TOK_ROWS]
    loads[3].wait()
    width = w.shape[1] // 2
    attended = att[...].T

    def columns(first):
        return jnp.dot(attended, w[:, pl.ds(pl.multiple_of(first, width), width)], preferred_element_type=jnp.float32)

    away[...] = columns((1 - head) * width).astype(jnp.bfloat16)
    over_heads = send(away, got, "head")
    kept_out[...] = columns(head * width)
    vals_z = next_hops(vals_z, vals_2, "z", Z_SECOND, 3)
    over_heads.wait_recv()
    mixed[...] = (kept_out[...] + got[...].astype(jnp.float32)).astype(jnp.bfloat16)

    arrived(vals_z)
    sent(vals_from)
    crossing = between_cores(vals_st, vals_3, VALS_COL + 4, vals_pools[:3])
    crossing.wait_recv()
    sent([crossing])
    sent([swap_vals])
    pick(vals_in, BLK_DEV, picks, VALS_COL + 5, vals_pools)
    vals_out = pltpu.make_async_copy(vals_in, decoded.at[:, 1], local_sem.at[4])
    vals_out.start()
    swap_keys.wait_recv()
    keys_out = pltpu.make_async_copy(keys_end, decoded.at[:, 0], local_sem.at[5])
    keys_out.start()
    vals_out.wait()
    keys_out.wait()
    sent(sends[:])


def move_and_multiply(picks, spread, kv_own, limits, weight, blocks):
    local_kv, rows, _ = spread.shape
    half = lambda n: pltpu.VMEM((n,) + blocks.shape[2:], blocks.dtype)
    vmem, hbm = pl.BlockSpec(memory_space=pltpu.VMEM), pl.BlockSpec(memory_space=pl.ANY)
    width = weight.shape[1] // 2
    return pl.pallas_call(
        move_kernel,
        out_shape=(
            jax.ShapeDtypeStruct((TOK_ROWS, width), jnp.bfloat16),
            jax.ShapeDtypeStruct(blocks.shape, blocks.dtype),
        ),
        in_specs=[pl.BlockSpec(memory_space=pltpu.SMEM), vmem, hbm, vmem, hbm, hbm],
        out_specs=(vmem, hbm),
        scratch_shapes=[
            pltpu.VMEM((SHARDS,) + kv_own.shape, jnp.bfloat16),
            pltpu.VMEM(weight.shape, jnp.bfloat16),
            half(BLK_DEV), half(BLK_DEV), half(BLK_DEV),
            half(2 * max(Z_FIRST[0], Y_SECOND[0])), half(2 * sum(Z_FIRST)), half(2 * sum(Y_SECOND)), half(BLK_DEV), half(BLK_DEV),
            half(2 * max(Y_FIRST[0], Z_SECOND[0])), half(2 * sum(Y_FIRST)), half(2 * sum(Z_SECOND)), half(BLK_DEV),
            pltpu.VMEM((8, rows), jnp.float32),
            pltpu.VMEM((8, rows), jnp.float32),
            pltpu.VMEM((local_kv, HD, rows), jnp.float32),
            pltpu.VMEM((weight.shape[0], TOK_ROWS), jnp.bfloat16),
            pltpu.VMEM((TOK_ROWS, width), jnp.float32),
            pltpu.VMEM((TOK_ROWS, width), jnp.bfloat16),
            pltpu.VMEM((TOK_ROWS, width), jnp.bfloat16),
            pltpu.SemaphoreType.DMA((6,)),
            pltpu.SemaphoreType.DMA((N_COPIES,)),
            pltpu.SemaphoreType.DMA((N_COPIES,)),
        ],
        compiler_params=pltpu.CompilerParams(
            collective_id=0, has_side_effects=True, vmem_limit_bytes=63 * 1024 * 1024
        ),
        cost_estimate=pl.CostEstimate(flops=10**10, bytes_accessed=20 * 2**20, transcendentals=10**7),
    )(picks, spread, kv_own, limits, weight, blocks)


def per_device(queries, keyvals, span_req, prefill_blocks, block_dest, out_weight):
    tok_rows = queries.shape[1]
    local_kv = keyvals.shape[3] // HD
    group = HEADS // KVH
    tok = (lax.axis_index("y") * NZ + lax.axis_index("z")) * NC + lax.axis_index("core")
    first_query = tok * tok_rows
    segments = span_req[0]

    picks, room = plan(block_dest)
    own_segments = lax.dynamic_slice_in_dim(segments, first_query, tok_rows)
    starts = jnp.sum(segments[None, :] < own_segments[:, None], axis=1).astype(jnp.int32)
    places = first_query + jnp.arange(tok_rows, dtype=jnp.int32)
    limits = jnp.stack([jnp.tile(starts, group), jnp.tile(places, group)])
    scaled = queries[0].reshape(tok_rows, local_kv, group, HD) * jnp.bfloat16(1.0 / math.sqrt(HD))
    own = jnp.eye(local_kv, dtype=jnp.bfloat16)
    spread = jnp.einsum("qcgd,ce->cgqed", scaled, own).reshape(local_kv, group * tok_rows, local_kv * HD)
    kv_own = keyvals[0].reshape(tok_rows, 2 * local_kv * HD)
    mixed, routed = move_and_multiply(picks, spread, kv_own, limits, out_weight, prefill_blocks)
    decode_blocks = lax.cond(
        room[0, 0] <= 0.0,
        lambda done, blocks, dest: done,
        lambda done, blocks, dest: hand_over_padded(blocks, dest),
        routed, prefill_blocks, block_dest,
    )
    return mixed[None], decode_blocks


def solution(mesh):
    fine = Mesh(mesh.devices.reshape(2, NY, NZ, NC, 2), ("section",) + TOK + ("head",))
    return jax.shard_map(
        per_device,
        mesh=fine,
        in_specs=(
            P("section", TOK, "head"),
            P("section", TOK, None, "head"),
            P("section", None),
            P(("section",) + TOK, None, None, "head"),
            P(),
            P("head", None),
        ),
        out_specs=(P("section", TOK, "head"), P(("section",) + TOK, None, None, "head")),
        check_vma=False,
    )
```

```python
import functools
import math

import jax
import jax.numpy as jnp
from jax import lax
from jax.experimental import pallas as pl
from jax.experimental.pallas import tpu as pltpu
from jax.sharding import Mesh
from jax.sharding import PartitionSpec as P

HEADS = 32
KVH = 8
HD = 64
NY, NZ, NC = 4, 8, 2
BLK_DEV = 24
LONGEST = 6144
SHARDS = NY * NZ * NC
TOK = ("y", "z", "core")

Z_FIRST = (17, 13, 10, 4)
Y_SECOND = (18, 8)
Y_FIRST = (15, 7)
Z_SECOND = (20, 15, 11, 4)


def pack_rows(blocks, dest_list, shard_count):
    targets = jnp.arange(shard_count, dtype=jnp.int32)
    matches = dest_list[None, :] == targets[:, None]
    present = jnp.any(matches, axis=1)
    picked = jnp.argmax(matches, axis=1)
    chosen = jnp.take(blocks, picked, axis=0)
    return jnp.where(present[:, None, None, None], chosen, jnp.zeros_like(chosen))


def compact_rows(received, sender_table, receiver, per_shard):
    present = jnp.any(sender_table == receiver, axis=1)
    ranking = jnp.cumsum(present.astype(jnp.int32)) - 1
    slot_ids = jnp.arange(per_shard, dtype=jnp.int32)
    matches = (ranking[None, :] == slot_ids[:, None]) & present[None, :]
    picked = jnp.argmax(matches, axis=1)
    return jnp.take(received, picked, axis=0)


def hand_over_padded(prefill_blocks, block_dest):
    per_shard = prefill_blocks.shape[0]
    section = lax.axis_index("section")
    tok = (lax.axis_index("y") * NZ + lax.axis_index("z")) * NC + lax.axis_index("core")
    dest_table = block_dest.reshape(-1, SHARDS, per_shard)
    moved = lax.ppermute(prefill_blocks, "section", [(0, 1), (1, 0)])
    sender_table = lax.dynamic_index_in_dim(dest_table, 1 - section, 0, keepdims=False)
    dest_list = lax.dynamic_index_in_dim(sender_table, tok, 0, keepdims=False)
    sending = pack_rows(moved, dest_list % SHARDS, SHARDS)
    received = lax.all_to_all(sending, TOK, split_axis=0, concat_axis=0, tiled=True)
    return compact_rows(received, sender_table, section * SHARDS + tok, per_shard)


LANES = 32
POOL = 256
KEYS_COL, VALS_COL = 0, 8


def count_dot(a, b):
    return jnp.dot(a.astype(jnp.bfloat16), b.astype(jnp.bfloat16), preferred_element_type=jnp.float32)


def forward_share(number, ring, cap):
    half = ring // 2
    plus, minus, far = sum(number[1:half]), sum(number[half + 1 :]), number[half]
    even = jnp.floor((far + minus - plus + 1.0) * 0.5)
    return jnp.clip(even, jnp.maximum(0.0, far - cap), jnp.minimum(far, cap * 1.0))


def ring_lists(step, valid, before_of, total_of, ring, caps):
    half = ring // 2
    hot = [None] + [jnp.where(valid & (step == k), 1.0, 0.0) for k in range(1, ring)]
    tall = jnp.concatenate(hot[1:], axis=0)
    rows = step.shape[0]
    parts = lambda a: [None] + [a[k * rows : (k + 1) * rows] for k in range(ring - 1)]
    before, total = parts(count_dot(tall, before_of)), parts(count_dot(tall, total_of))
    number = [0.0] + total[1:]
    share = forward_share(number, ring, caps[-1])
    ahead_mask, back_mask = jnp.zeros_like(share), jnp.zeros_like(share)
    rank, spot = jnp.zeros_like(share), jnp.zeros_like(share)
    ahead_at = [sum(caps[:k]) for k in range(half)]
    back_at = [sum(caps) + at for at in ahead_at]
    far_ahead = hot[half] * jnp.where(before[half] < share, 1.0, 0.0)
    far_back = hot[half] - far_ahead
    for mask, place, at in (
        (far_ahead, before[half], ahead_at[half - 1]),
        (far_back, before[half] - share, back_at[half - 1]),
    ):
        rank += mask * place
        spot += mask * (place + at)
    ahead_mask += far_ahead
    back_mask += far_back
    for k in range(1, half):
        place = sum(number[k + 1 : half]) + share + before[k]
        rank += hot[k] * place
        spot += hot[k] * (place + ahead_at[k - 1])
        ahead_mask += hot[k]
        place = sum(number[half + 1 : ring - k]) + number[half] - share + before[ring - k]
        rank += hot[ring - k] * place
        spot += hot[ring - k] * (place + back_at[k - 1])
        back_mask += hot[ring - k]
    return ahead_mask, back_mask, rank, spot


def list_column(mask, rank, spot):
    slot = jnp.sum(mask * (rank + 1.0), axis=0, keepdims=True)
    code = jnp.sum(mask * spot, axis=0, keepdims=True)
    want = lax.broadcasted_iota(jnp.int32, (32, 1), 0).astype(jnp.float32) + 1.0
    return jnp.sum(jnp.where(slot == want, code, 0.0), axis=1, keepdims=True)


def wide_column(mask, rank, spot):
    want = lax.broadcasted_iota(jnp.int32, (32, 1), 0).astype(jnp.float32) + 1.0
    slot, code = mask * (rank + 1.0), mask * spot
    total = jnp.zeros((32, 1), jnp.float32)
    for row in range(mask.shape[0]):
        hit = slot[row : row + 1, :] == want
        total += jnp.sum(jnp.where(hit, code[row : row + 1, :], 0.0), axis=1, keepdims=True)
    return total


def route_plan(dest, other, y_first, me_y, me_z, core):
    rows, lanes = dest.shape
    ring_1, caps_1, ring_2, caps_2 = (NY, Y_FIRST, NZ, Z_SECOND) if y_first else (NZ, Z_FIRST, NY, Y_SECOND)
    me_1, me_2 = (me_y, me_z) if y_first else (me_z, me_y)
    lane = lax.broadcasted_iota(jnp.int32, (rows, lanes), 1)
    row = lax.broadcasted_iota(jnp.int32, (rows, lanes), 0)
    at_1, index = lane // LANES, (lane % LANES).astype(jnp.float32)
    valid = dest >= 0
    dest_y, dest_z = dest // (NZ * NC), dest // NC % NZ
    dest_1, dest_2 = (dest_y, dest_z) if y_first else (dest_z, dest_y)
    left = lax.broadcasted_iota(jnp.int32, (lanes, lanes), 0)
    right = lax.broadcasted_iota(jnp.int32, (lanes, lanes), 1)
    same = left // LANES == right // LANES
    one = lambda a: jnp.where(a, 1.0, 0.0)
    earlier = one(left < right)
    same_earlier, same_all = one(same & (left < right)), one(same)
    group_earlier = one(left // LANES < right // LANES)

    ahead, back, rank, spot = ring_lists(
        (dest_1 - at_1) & (ring_1 - 1), valid, same_earlier, same_all, ring_1, caps_1
    )
    own = one((row == me_2) & (at_1 == me_1))
    columns = [list_column(ahead * own, rank, index), list_column(back * own, rank, index)]
    moved = ahead + back
    spot_1 = jnp.where(moved > 0.5, POOL + spot, index)

    ahead, back, rank, spot = ring_lists(
        (dest_2 - row) & (ring_2 - 1), valid & (dest_1 == me_1), earlier, jnp.ones_like(earlier), ring_2, caps_2
    )
    own = one(row == me_2)
    columns += [list_column(ahead * own, rank, spot_1), list_column(back * own, rank, spot_1)]
    moved = ahead + back
    spot_2 = jnp.where(moved > 0.5, 2 * POOL + spot, spot_1)

    me = (me_y * NZ + me_z) * NC + core
    mine, theirs, far = one(dest == me), one(dest == me + 1 - 2 * core), one(other == me)

    def earlier_chips(hot):
        per_chip = count_dot(hot, same_all)
        if not y_first:
            below = jnp.zeros_like(hot)
            line = jnp.sum(hot, axis=1, keepdims=True)
            for r in range(rows):
                below += jnp.where(row > r, line[r : r + 1, :], 0.0)
            return below + count_dot(hot, group_earlier), per_chip
        below = jnp.zeros_like(hot)
        for r in range(rows):
            below += jnp.where(row > r, per_chip[r : r + 1, :], 0.0)
        whole = jnp.sum(hot, axis=0, keepdims=True)
        return below + count_dot(jnp.broadcast_to(whole, hot.shape), group_earlier), per_chip

    mine_at, mine_in = earlier_chips(mine)
    theirs_at, _ = earlier_chips(theirs)
    far_at, far_in = earlier_chips(far)
    second = core.astype(jnp.float32)
    columns.append(wide_column(theirs, theirs_at, spot_2))
    columns.append(
        wide_column(mine, mine_at + far_at + second * far_in, spot_2)
        + wide_column(far, mine_at + far_at + (1.0 - second) * mine_in, 3 * POOL + far_at)
    )
    return columns


def over_room(number, ring, caps):
    half = ring // 2
    share = forward_share(number, ring, caps[-1])
    worst = jnp.full_like(share, -1.0)
    for k in range(1, half + 1):
        ahead = sum(number[k:half]) + share
        back = sum(number[half + 1 : ring - k + 1]) + number[half] - share
        worst = jnp.maximum(worst, jnp.maximum(ahead, back) - caps[k - 1])
    return worst


def list_room(dest, y_first):
    rows, lanes = dest.shape
    ring_1, caps_1, ring_2, caps_2 = (NY, Y_FIRST, NZ, Z_SECOND) if y_first else (NZ, Z_FIRST, NY, Y_SECOND)
    lane = lax.broadcasted_iota(jnp.int32, (rows, lanes), 1)
    row = lax.broadcasted_iota(jnp.int32, (rows, lanes), 0)
    valid = dest >= 0
    dest_y, dest_z = dest // (NZ * NC), dest // NC % NZ
    dest_1, dest_2 = (dest_y, dest_z) if y_first else (dest_z, dest_y)
    step_1 = (dest_1 - lane // LANES) & (ring_1 - 1)
    step_2 = (dest_2 - row) & (ring_2 - 1)
    left = lax.broadcasted_iota(jnp.int32, (lanes, lanes), 0)
    right = lax.broadcasted_iota(jnp.int32, (lanes, lanes), 1)
    same = jnp.where(left // LANES == right // LANES, 1.0, 0.0)
    tall = jnp.concatenate([jnp.where(valid & (step_1 == k), 1.0, 0.0) for k in range(1, ring_1)], axis=0)
    tall = count_dot(tall, same)
    number = [0.0] + [tall[k * rows : (k + 1) * rows] for k in range(ring_1 - 1)]
    worst = jnp.max(over_room(number, ring_1, caps_1))
    for to in range(ring_1):
        here = valid & (dest_1 == to)
        number = [0.0] + [
            jnp.sum(jnp.where(here & (step_2 == k), 1.0, 0.0), axis=1, keepdims=True) for k in range(1, ring_2)
        ]
        worst = jnp.maximum(worst, jnp.max(over_room(number, ring_2, caps_2)))
    return worst


def plan_kernel(by_y, by_z, picks, room):
    section, core = lax.axis_index("section"), lax.axis_index("core")
    me_y, me_z = lax.axis_index("y"), lax.axis_index("z")
    keys = route_plan(by_y[section, core], by_y[section, 1 - core], False, me_y, me_z, core)
    vals = route_plan(by_z[1 - section, core], by_z[1 - section, 1 - core], True, me_y, me_z, core)
    lane = lax.broadcasted_iota(jnp.int32, (32, 128), 1)
    table = jnp.zeros((32, 128), jnp.float32)
    for base, columns in ((KEYS_COL, keys), (VALS_COL, vals)):
        for at, column in enumerate(columns):
            table = jnp.where(lane == base + at, column, table)
    picks[...] = table.astype(jnp.int32)
    worst = jnp.float32(-1.0)
    for half in range(2):
        for c in range(NC):
            worst = jnp.maximum(worst, list_room(by_y[half, c], False))
            worst = jnp.maximum(worst, list_room(by_z[half, c], True))
    room[...] = jnp.full(room.shape, worst, jnp.float32)


def plan_tables(block_dest):
    tables = (block_dest % SHARDS).reshape(2, NY, NZ, NC, BLK_DEV)
    tables = jnp.pad(tables, ((0, 0),) * 4 + ((0, LANES - BLK_DEV),), constant_values=-1)
    by_y = jnp.pad(
        tables.transpose(0, 3, 1, 2, 4).reshape(2, NC, NY, NZ * LANES),
        ((0, 0), (0, 0), (0, 8 - NY), (0, 0)), constant_values=-1,
    )
    by_z = tables.transpose(0, 3, 2, 1, 4).reshape(2, NC, NZ, NY * LANES)
    return by_y, by_z


def plan(block_dest):
    vmem = pl.BlockSpec(memory_space=pltpu.VMEM)
    return pl.pallas_call(
        plan_kernel,
        out_shape=(jax.ShapeDtypeStruct((32, 128), jnp.int32), jax.ShapeDtypeStruct((8, 128), jnp.float32)),
        in_specs=[vmem, vmem],
        out_specs=(vmem, vmem),
    )(*plan_tables(block_dest))


UNIT = 1024
SLAB = UNIT // NC
TOK_ROWS = 128
PARTS = 2
REQUESTS = 16


RATE = {"x": 0.0475, "y": 0.0475, "z": 0.0475, "core": 0.24, "head": 0.0475}
LATENCY = 1.8
DEPTH = {"x": 1, "y": 1, "z": 2, "core": 4, "head": 1}
FIRST_Z = {"tokens": 0, "keys0": 1, "vals0": 2, "keys1": 3, "vals1": 4}
FIRST_Y = {"tokens": 0, "vals0": 1, "far": 1.5, "keys0": 2, "vals1": 3, "keys1": 4}
UNIT_US = 5.7
SLACK = 3.0


class Transfer:
    def __init__(self, link, megabytes, *moves, small=False):
        self.link, self.megabytes, self.moves, self.small = link, megabytes, moves, small
        self.copies, self.ends, self.left = None, None, megabytes


class Order:
    def __init__(self, send):
        self.send, self.now = send, 0.0
        self.queues = {link: [] for link in RATE}
        self.busy = {link: [] for link in RATE}
        self.seen = dict.fromkeys(RATE, 0.0)

    def advance(self, link):
        while self.busy[link]:
            span = min(t.left for t in self.busy[link]) * len(self.busy[link]) / RATE[link]
            ended = self.seen[link] + span <= self.now
            span = min(span, self.now - self.seen[link])
            part = span * RATE[link] / len(self.busy[link])
            for t in self.busy[link]:
                t.left -= part
            self.seen[link] += span
            if not ended:
                break
            self.busy[link] = [t for t in self.busy[link] if t.left > 1e-9]
        self.seen[link] = self.now

    def foresee(self, link):
        at, gone = self.now, 0.0
        todo = sorted(self.busy[link], key=lambda t: t.left)
        for rank, t in enumerate(todo):
            at += (t.left - gone) * (len(todo) - rank) / RATE[link]
            gone = t.left
            t.ends = at

    def post(self, transfer, rank):
        self.queues[transfer.link].append((rank, transfer))
        self.issue()

    def issue(self):
        for link, queue in self.queues.items():
            self.advance(link)
            while queue and (len(self.busy[link]) < DEPTH[link] or min(queue, key=lambda e: e[0])[1].small):
                entry = min(queue, key=lambda e: e[0])
                queue.remove(entry)
                self.busy[link].append(entry[1])
                entry[1].copies = [self.send(*move) for move in entry[1].moves]
            self.foresee(link)

    def run(self, chains):
        waiting = []

        def step(name, chain):
            for wanted in chain:
                if wanted is None:
                    waiting.append((name, None, chain))
                    return
                if wanted.copies is None and all(wanted is not t for q in self.queues.values() for _, t in q):
                    rank = (FIRST_Y if wanted.link == "y" else FIRST_Z).get(name, 9)
                    self.post(wanted, rank)
                waiting.append((name, wanted, chain))
                return

        for name, chain in chains:
            step(name, chain)
        while waiting:
            self.issue()
            ready = [w for w in waiting if w[1] is not None and w[1].ends is not None]
            compute = [w for w in waiting if w[1] is None]
            first = min(ready, key=lambda w: w[1].ends) if ready else None
            if compute and (first is None or first[1].ends + LATENCY - self.now > SLACK):
                entry = compute[0]
                self.now += UNIT_US
            elif first is not None:
                entry = first
                self.now = max(self.now, first[1].ends + LATENCY)
                for copy in first[1].copies:
                    copy.wait_recv()
            else:
                self.now = min(t.ends for busy in self.busy.values() for t in busy) + 1e-6
                continue
            waiting = [w for w in waiting if w is not entry]
            step(entry[0], entry[2])


def pick(dst, first, count, picks, column, pools):
    def one(j, carry):
        code = picks[j, column]
        block = None
        for at, pool in enumerate(pools):
            row = jnp.clip(code - at * POOL, 0, pool.shape[0] - 1)
            found = pool[row]
            block = found if block is None else jnp.where(code >= at * POOL, found, block)
        dst[first + j] = block
        return carry

    lax.fori_loop(0, count, one, 0)


def move_kernel(picks, queries, kv_own, requests, weight, blocks, mixed, decoded, *scratch):
    kv, w, spread, high, total, accum, att, kept_out, away, got, local_sem, send_sem, recv_sem = scratch[:13]
    buffers = scratch[13:]
    section, core, head = lax.axis_index("section"), lax.axis_index("core"), lax.axis_index("head")
    y, z = lax.axis_index("y"), lax.axis_index("z")
    peers = {
        "x": {"section": 1 - section}, "core": {"core": 1 - core}, "head": {"head": 1 - head},
        "y+": {"y": (y + 1) % NY}, "y-": {"y": (y + NY - 1) % NY},
        "z+": {"z": (z + 1) % NZ}, "z-": {"z": (z + NZ - 1) % NZ},
    }
    count = [0, 0]
    sends = []

    def send(src, dst, to):
        at = count[0]
        count[0] += 1
        copy = pltpu.make_async_remote_copy(
            src_ref=src, dst_ref=dst, send_sem=send_sem.at[at], recv_sem=recv_sem.at[at],
            device_id=peers[to], device_id_type=pl.DeviceIdType.MESH,
        )
        copy.start()
        sends.append(copy)
        return copy

    def sent(copies):
        for copy in copies:
            copy.wait_send()
            sends[:] = [c for c in sends if c is not copy]

    def local(src, dst):
        copy = pltpu.make_async_copy(src, dst, local_sem.at[count[1]])
        count[1] += 1
        copy.start()
        return copy

    part_rows = blocks.shape[2] // PARTS
    slot = part_rows * blocks.shape[3] * 2e-6

    def rows_of(ref, kind, part):
        return ref.at[:, kind, pl.ds(part * part_rows, part_rows)]

    def shard_at(c, yy, zz):
        return (c * NY + yy) * NZ + zz

    own = kv.at[shard_at(core, y, z)]
    parts = [buffers[p * 12 : (p + 1) * 12] for p in range(PARTS)]
    load_kv = local(kv_own, own)
    load_vals = [local(rows_of(blocks, 1, p), parts[p][1]) for p in range(PARTS)]
    load_keys = [local(rows_of(blocks, 0, p), parts[p][0]) for p in range(PARTS)]
    load_weight = local(weight, w)
    barrier = pltpu.get_barrier_semaphore()
    for peer in peers.values():
        pl.semaphore_signal(barrier, inc=1, device_id=peer, device_id_type=pl.DeviceIdType.MESH)
    pl.semaphore_wait(barrier, len(peers))

    def around(stage, arrivals, axis, caps, column, pools):
        cap, back = caps[0], sum(caps)
        ways = ((0, axis + "+", 0), (1, axis + "-", back))
        for at, to, base in ways:
            pick(stage, at * cap, cap, picks, column + at, pools)
        from_stage = Transfer(axis, cap * slot, *[
            (stage.at[pl.ds(at * cap, cap)], arrivals.at[pl.ds(base, cap)], to) for at, to, base in ways
        ])
        yield from_stage
        for k in range(1, len(caps)):
            came, at = sum(caps[: k - 1]), sum(caps[:k])
            yield Transfer(axis, caps[k] * slot, *[
                (arrivals.at[pl.ds(base + came, caps[k])], arrivals.at[pl.ds(base + at, caps[k])], to)
                for _, to, base in ways
            ])
        sent(from_stage.copies)

    def between_cores(stage, arrivals, column, pools):
        pick(stage, 0, BLK_DEV, picks, column, pools)
        crossing = Transfer("core", BLK_DEV * slot, (stage.at[pl.ds(0, BLK_DEV)], arrivals, "core"))
        yield crossing
        sent(crossing.copies)

    outs = []

    def keys_chain(part):
        held, _, _, stage, came_1, came_2, came_3, last = parts[part][:8]
        load_keys[part].wait()
        yield from around(stage, came_1, "z", Z_FIRST, KEYS_COL, [held])
        yield from around(stage, came_2, "y", Y_SECOND, KEYS_COL + 2, [held, came_1])
        yield from between_cores(stage, came_3, KEYS_COL + 4, [held, came_1, came_2])
        pick(stage, 0, BLK_DEV, picks, KEYS_COL + 5, [held, came_1, came_2, came_3])
        yield Transfer("x", BLK_DEV * slot, (stage.at[pl.ds(0, BLK_DEV)], last, "x"))
        outs.append(local(last, rows_of(decoded, 0, part)))

    def vals_chain(part):
        _, inside, held = parts[part][:3]
        stage, came_1, came_2, came_3 = parts[part][8:]
        load_vals[part].wait()
        swap = Transfer("x", BLK_DEV * slot, (inside, held, "x"))
        yield swap
        yield from around(stage, came_1, "y", Y_FIRST, VALS_COL, [held])
        yield from around(stage, came_2, "z", Z_SECOND, VALS_COL + 2, [held, came_1])
        yield from between_cores(stage, came_3, VALS_COL + 4, [held, came_1, came_2])
        sent(swap.copies)
        pick(inside, 0, BLK_DEV, picks, VALS_COL + 5, [held, came_1, came_2, came_3])
        outs.append(local(inside, rows_of(decoded, 1, part)))

    first_query = ((y * NZ + z) * NC + core) * TOK_ROWS
    local_kv, rows, _ = spread.shape
    group = rows // TOK_ROWS

    def row_limits():
        tile_of = requests[pl.ds((y * NZ + z) * NC + core, 1), :]
        starts = jnp.zeros(tile_of.shape, jnp.float32)
        for r in range(1, REQUESTS):
            earlier = jnp.where(requests[...] < r, 1.0, 0.0)
            first = jnp.sum(jnp.sum(earlier, axis=1, keepdims=True), axis=0, keepdims=True)
            starts = jnp.where(tile_of == r, first, starts)
        places = (lax.broadcasted_iota(jnp.int32, tile_of.shape, 1) + first_query).astype(jnp.float32)
        return jnp.concatenate([starts] * group, axis=1), jnp.concatenate([places] * group, axis=1)

    def prepare():
        high[...] = jnp.full_like(high, -1e30)
        total[...] = jnp.zeros_like(total)
        accum[...] = jnp.zeros_like(accum)
        spread[...] = jnp.zeros_like(spread)
        for c in range(local_kv):
            for g in range(group):
                at = (c * group + g) * HD
                spread[c, g * TOK_ROWS : (g + 1) * TOK_ROWS, c * HD : (c + 1) * HD] = queries[
                    :, at : at + HD
                ] * jnp.bfloat16(1.0 / math.sqrt(HD))
        starts, places = row_limits()
        high[4:5, :] = starts
        high[5:6, :] = places

    def slab(half):
        unit, of_core = half // NC, half % NC
        at = shard_at(of_core, 0, 0) + unit * (SLAB // TOK_ROWS)
        block = kv[pl.ds(at, SLAB // TOK_ROWS)].reshape(SLAB, kv.shape[2])
        keys, vals = block[:, : local_kv * HD], block[:, local_kv * HD :].T
        row = lax.broadcasted_iota(jnp.int32, (SLAB, rows), 0)
        pos = unit * UNIT + of_core * TOK_ROWS + (row // TOK_ROWS) * (NC * TOK_ROWS) + row % TOK_ROWS
        pos = pos.astype(jnp.float32)
        keep = (pos >= high[4:5, :]) & (pos <= high[5:6, :])
        for c in range(local_kv):
            scores = lax.dot_general(
                keys, spread[c], (((1,), (1,)), ((), ())), preferred_element_type=jnp.float32
            )
            scores = jnp.where(keep, scores, -1e30)
            before = high[c : c + 1, :]
            now = jnp.maximum(before, jnp.max(scores, axis=0, keepdims=True))
            expo = jnp.exp(scores - now)
            factor = jnp.exp(before - now)
            high[c : c + 1, :] = now
            total[c : c + 1, :] = total[c : c + 1, :] * factor + jnp.sum(expo, axis=0, keepdims=True)
            accum[c] = accum[c] * factor + jnp.dot(
                vals[c * HD : (c + 1) * HD], expo.astype(jnp.bfloat16), preferred_element_type=jnp.float32
            )

    def units(low, top):
        def one(half, carry):
            start = half // NC * UNIT

            @pl.when((start < first_query + TOK_ROWS) & (start + UNIT > first_query - (LONGEST - 1)))
            def _():
                slab(half)

            return carry

        lax.fori_loop(low * NC, top * NC, one, 0)

    def tokens_chain():
        shard = kv_own.shape[0] * kv_own.shape[1] * 2e-6
        load_kv.wait()
        yield Transfer("z", shard, (own, own, "z+"), (own, own, "z-"), small=True)
        for k in range(1, NZ // 2):
            ahead = kv.at[shard_at(core, y, (z - k + NZ) % NZ)]
            back = kv.at[shard_at(core, y, (z + k) % NZ)]
            moves = [(ahead, ahead, "z+")]
            if k < NZ // 2 - 1:
                moves.append((back, back, "z-"))
            yield Transfer("z", shard, *moves, small=True)

        def line(yy):
            return kv.at[pl.ds(shard_at(core, yy, 0), NZ)]

        def some(yy, first):
            return kv.at[pl.ds(shard_at(core, yy, first), NZ // 2)]

        def to_core(yy):
            crossing = Transfer("core", NZ * shard, (line(yy), line(yy), "core"))
            order.post(crossing, 0)
            return crossing

        over, under, across = (y + 1) % NY, (y + NY - 1) % NY, (y + 2) % NY
        around_y = Transfer("y", NZ * shard, (line(y), line(y), "y+"), (line(y), line(y), "y-"))
        order.post(around_y, FIRST_Y["tokens"])
        crossings = [to_core(y)]
        prepare()
        yield around_y
        far = Transfer(
            "y", NZ // 2 * shard,
            (some(under, 0), some(under, 0), "y+"), (some(over, NZ // 2), some(over, NZ // 2), "y-"),
        )
        order.post(far, FIRST_Y["far"])
        crossings += [to_core(under), to_core(over)]
        yield far
        crossings.append(to_core(across))
        for crossing in crossings:
            yield crossing
        for unit in range(kv.shape[0] * TOK_ROWS // UNIT):
            yield None
            units(unit, unit + 1)

        for c in range(local_kv):
            done = (accum[c] / total[c : c + 1, :]).astype(jnp.bfloat16)
            for g in range(group):
                at = (c * group + g) * HD
                att[at : at + HD, :] = done[:, g * TOK_ROWS : (g + 1) * TOK_ROWS]
        load_weight.wait()
        width = w.shape[1] // 2
        attended = att[...].T

        def columns(first):
            first = pl.multiple_of(first, width)
            return jnp.dot(attended, w[:, pl.ds(first, width)], preferred_element_type=jnp.float32)

        away[...] = columns((1 - head) * width).astype(jnp.bfloat16)
        over_heads = Transfer("head", 0.26, (away, got, "head"))
        order.post(over_heads, 0)
        kept_out[...] = columns(head * width)
        yield over_heads
        mixed[...] = (kept_out[...] + got[...].astype(jnp.float32)).astype(jnp.bfloat16)

    order = Order(send)
    chains = [("tokens", tokens_chain())]
    chains += [("vals%d" % part, vals_chain(part)) for part in range(PARTS)]
    chains += [("keys%d" % part, keys_chain(part)) for part in range(PARTS)]
    order.run(chains)
    for copy in outs:
        copy.wait()
    sent(sends[:])


def move_and_multiply(picks, queries, kv_own, requests, weight, blocks):
    local_kv = kv_own.shape[1] // (2 * HD)
    rows = HEADS // KVH * TOK_ROWS
    part_rows = blocks.shape[2] // PARTS
    half = lambda n: pltpu.VMEM((n, part_rows) + blocks.shape[3:], blocks.dtype)
    vmem, hbm = pl.BlockSpec(memory_space=pltpu.VMEM), pl.BlockSpec(memory_space=pl.ANY)
    width = weight.shape[1] // 2
    copies = 16 + PARTS * 28
    return pl.pallas_call(
        move_kernel,
        out_shape=(
            jax.ShapeDtypeStruct((TOK_ROWS, width), jnp.bfloat16),
            jax.ShapeDtypeStruct(blocks.shape, blocks.dtype),
        ),
        in_specs=[pl.BlockSpec(memory_space=pltpu.SMEM), vmem, hbm, vmem, hbm, hbm],
        out_specs=(vmem, hbm),
        scratch_shapes=[
            pltpu.VMEM((SHARDS,) + kv_own.shape, jnp.bfloat16),
            pltpu.VMEM(weight.shape, jnp.bfloat16),
            pltpu.VMEM((local_kv, rows, local_kv * HD), jnp.bfloat16),
            pltpu.VMEM((8, rows), jnp.float32),
            pltpu.VMEM((8, rows), jnp.float32),
            pltpu.VMEM((local_kv, HD, rows), jnp.float32),
            pltpu.VMEM((weight.shape[0], TOK_ROWS), jnp.bfloat16),
            pltpu.VMEM((TOK_ROWS, width), jnp.float32),
            pltpu.VMEM((TOK_ROWS, width), jnp.bfloat16),
            pltpu.VMEM((TOK_ROWS, width), jnp.bfloat16),
            pltpu.SemaphoreType.DMA((2 + 4 * PARTS,)),
            pltpu.SemaphoreType.DMA((copies,)),
            pltpu.SemaphoreType.DMA((copies,)),
        ]
        + [
            half(n)
            for _ in range(PARTS)
            for n in (
                BLK_DEV, BLK_DEV, BLK_DEV,
                2 * max(Z_FIRST[0], Y_SECOND[0]), 2 * sum(Z_FIRST), 2 * sum(Y_SECOND), BLK_DEV, BLK_DEV,
                2 * max(Y_FIRST[0], Z_SECOND[0]), 2 * sum(Y_FIRST), 2 * sum(Z_SECOND), BLK_DEV,
            )
        ],
        compiler_params=pltpu.CompilerParams(
            collective_id=0, has_side_effects=True, vmem_limit_bytes=63 * 1024 * 1024
        ),
        cost_estimate=pl.CostEstimate(flops=10**10, bytes_accessed=20 * 2**20, transcendentals=10**7),
    )(picks, queries, kv_own, requests, weight, blocks)


def per_device(queries, keyvals, span_req, prefill_blocks, block_dest, out_weight):
    picks, room = plan(block_dest)
    kv_own = keyvals[0].reshape(TOK_ROWS, -1)
    requests = span_req.reshape(SHARDS, TOK_ROWS)
    mixed, routed = move_and_multiply(picks, queries[0], kv_own, requests, out_weight, prefill_blocks)
    decode_blocks = lax.cond(
        room[0, 0] <= 0.0,
        lambda done, blocks, dest: done,
        lambda done, blocks, dest: hand_over_padded(blocks, dest),
        routed, prefill_blocks, block_dest,
    )
    return mixed[None], decode_blocks


def solution(mesh):
    fine = Mesh(mesh.devices.reshape(2, NY, NZ, NC, 2), ("section",) + TOK + ("head",))
    return jax.shard_map(
        per_device,
        mesh=fine,
        in_specs=(
            P("section", TOK, "head"),
            P("section", TOK, None, "head"),
            P("section", None),
            P(("section",) + TOK, None, None, "head"),
            P(),
            P("head", None),
        ),
        out_specs=(P("section", TOK, "head"), P(("section",) + TOK, None, None, "head")),
        check_vma=False,
    )
```

```python
import functools
import math

import jax
import jax.numpy as jnp
from jax import lax
from jax.experimental import pallas as pl
from jax.experimental.pallas import tpu as pltpu
from jax.sharding import Mesh
from jax.sharding import PartitionSpec as P

HEADS = 32
KVH = 8
HD = 64
NY, NZ, NC = 4, 8, 2
BLK_DEV = 24
LONGEST = 6144
SHARDS = NY * NZ * NC
TOK = ("y", "z", "core")

Z_FIRST = (17, 13, 10, 4)
Y_SECOND = (18, 8)
Y_FIRST = (15, 7)
Z_SECOND = (20, 15, 11, 4)


def pack_rows(blocks, dest_list, shard_count):
    targets = jnp.arange(shard_count, dtype=jnp.int32)
    matches = dest_list[None, :] == targets[:, None]
    present = jnp.any(matches, axis=1)
    picked = jnp.argmax(matches, axis=1)
    chosen = jnp.take(blocks, picked, axis=0)
    return jnp.where(present[:, None, None, None], chosen, jnp.zeros_like(chosen))


def compact_rows(received, sender_table, receiver, per_shard):
    present = jnp.any(sender_table == receiver, axis=1)
    ranking = jnp.cumsum(present.astype(jnp.int32)) - 1
    slot_ids = jnp.arange(per_shard, dtype=jnp.int32)
    matches = (ranking[None, :] == slot_ids[:, None]) & present[None, :]
    picked = jnp.argmax(matches, axis=1)
    return jnp.take(received, picked, axis=0)


def hand_over_padded(prefill_blocks, block_dest):
    per_shard = prefill_blocks.shape[0]
    section = lax.axis_index("section")
    tok = (lax.axis_index("y") * NZ + lax.axis_index("z")) * NC + lax.axis_index("core")
    dest_table = block_dest.reshape(-1, SHARDS, per_shard)
    moved = lax.ppermute(prefill_blocks, "section", [(0, 1), (1, 0)])
    sender_table = lax.dynamic_index_in_dim(dest_table, 1 - section, 0, keepdims=False)
    dest_list = lax.dynamic_index_in_dim(sender_table, tok, 0, keepdims=False)
    sending = pack_rows(moved, dest_list % SHARDS, SHARDS)
    received = lax.all_to_all(sending, TOK, split_axis=0, concat_axis=0, tiled=True)
    return compact_rows(received, sender_table, section * SHARDS + tok, per_shard)


LANES = 32
POOL = 256
KEYS_COL, VALS_COL = 0, 8


def count_dot(a, b):
    return jnp.dot(a.astype(jnp.bfloat16), b.astype(jnp.bfloat16), preferred_element_type=jnp.float32)


def forward_share(number, ring, cap):
    half = ring // 2
    plus, minus, far = sum(number[1:half]), sum(number[half + 1 :]), number[half]
    even = jnp.floor((far + minus - plus + 1.0) * 0.5)
    return jnp.clip(even, jnp.maximum(0.0, far - cap), jnp.minimum(far, cap * 1.0))


def ring_lists(step, valid, before_of, total_of, ring, caps):
    half = ring // 2
    hot = [None] + [jnp.where(valid & (step == k), 1.0, 0.0) for k in range(1, ring)]
    tall = jnp.concatenate(hot[1:], axis=0)
    rows = step.shape[0]
    parts = lambda a: [None] + [a[k * rows : (k + 1) * rows] for k in range(ring - 1)]
    before, total = parts(count_dot(tall, before_of)), parts(count_dot(tall, total_of))
    number = [0.0] + total[1:]
    share = forward_share(number, ring, caps[-1])
    ahead_mask, back_mask = jnp.zeros_like(share), jnp.zeros_like(share)
    rank, spot = jnp.zeros_like(share), jnp.zeros_like(share)
    ahead_at = [sum(caps[:k]) for k in range(half)]
    back_at = [sum(caps) + at for at in ahead_at]
    far_ahead = hot[half] * jnp.where(before[half] < share, 1.0, 0.0)
    far_back = hot[half] - far_ahead
    for mask, place, at in (
        (far_ahead, before[half], ahead_at[half - 1]),
        (far_back, before[half] - share, back_at[half - 1]),
    ):
        rank += mask * place
        spot += mask * (place + at)
    ahead_mask += far_ahead
    back_mask += far_back
    for k in range(1, half):
        place = sum(number[k + 1 : half]) + share + before[k]
        rank += hot[k] * place
        spot += hot[k] * (place + ahead_at[k - 1])
        ahead_mask += hot[k]
        place = sum(number[half + 1 : ring - k]) + number[half] - share + before[ring - k]
        rank += hot[ring - k] * place
        spot += hot[ring - k] * (place + back_at[k - 1])
        back_mask += hot[ring - k]
    return ahead_mask, back_mask, rank, spot


def list_column(mask, rank, spot):
    slot = jnp.sum(mask * (rank + 1.0), axis=0, keepdims=True)
    code = jnp.sum(mask * spot, axis=0, keepdims=True)
    want = lax.broadcasted_iota(jnp.int32, (32, 1), 0).astype(jnp.float32) + 1.0
    return jnp.sum(jnp.where(slot == want, code, 0.0), axis=1, keepdims=True)


def wide_column(mask, rank, spot):
    want = lax.broadcasted_iota(jnp.int32, (32, 1), 0).astype(jnp.float32) + 1.0
    slot, code = mask * (rank + 1.0), mask * spot
    total = jnp.zeros((32, 1), jnp.float32)
    for row in range(mask.shape[0]):
        hit = slot[row : row + 1, :] == want
        total += jnp.sum(jnp.where(hit, code[row : row + 1, :], 0.0), axis=1, keepdims=True)
    return total


def route_plan(dest, other, y_first, me_y, me_z, core):
    rows, lanes = dest.shape
    ring_1, caps_1, ring_2, caps_2 = (NY, Y_FIRST, NZ, Z_SECOND) if y_first else (NZ, Z_FIRST, NY, Y_SECOND)
    me_1, me_2 = (me_y, me_z) if y_first else (me_z, me_y)
    lane = lax.broadcasted_iota(jnp.int32, (rows, lanes), 1)
    row = lax.broadcasted_iota(jnp.int32, (rows, lanes), 0)
    at_1, index = lane // LANES, (lane % LANES).astype(jnp.float32)
    valid = dest >= 0
    dest_y, dest_z = dest // (NZ * NC), dest // NC % NZ
    dest_1, dest_2 = (dest_y, dest_z) if y_first else (dest_z, dest_y)
    left = lax.broadcasted_iota(jnp.int32, (lanes, lanes), 0)
    right = lax.broadcasted_iota(jnp.int32, (lanes, lanes), 1)
    same = left // LANES == right // LANES
    one = lambda a: jnp.where(a, 1.0, 0.0)
    earlier = one(left < right)
    same_earlier, same_all = one(same & (left < right)), one(same)
    group_earlier = one(left // LANES < right // LANES)

    ahead, back, rank, spot = ring_lists(
        (dest_1 - at_1) & (ring_1 - 1), valid, same_earlier, same_all, ring_1, caps_1
    )
    own = one((row == me_2) & (at_1 == me_1))
    columns = [list_column(ahead * own, rank, index), list_column(back * own, rank, index)]
    moved = ahead + back
    spot_1 = jnp.where(moved > 0.5, POOL + spot, index)

    ahead, back, rank, spot = ring_lists(
        (dest_2 - row) & (ring_2 - 1), valid & (dest_1 == me_1), earlier, jnp.ones_like(earlier), ring_2, caps_2
    )
    own = one(row == me_2)
    columns += [list_column(ahead * own, rank, spot_1), list_column(back * own, rank, spot_1)]
    moved = ahead + back
    spot_2 = jnp.where(moved > 0.5, 2 * POOL + spot, spot_1)

    me = (me_y * NZ + me_z) * NC + core
    mine, theirs, far = one(dest == me), one(dest == me + 1 - 2 * core), one(other == me)

    def earlier_chips(hot):
        per_chip = count_dot(hot, same_all)
        if not y_first:
            below = jnp.zeros_like(hot)
            line = jnp.sum(hot, axis=1, keepdims=True)
            for r in range(rows):
                below += jnp.where(row > r, line[r : r + 1, :], 0.0)
            return below + count_dot(hot, group_earlier), per_chip
        below = jnp.zeros_like(hot)
        for r in range(rows):
            below += jnp.where(row > r, per_chip[r : r + 1, :], 0.0)
        whole = jnp.sum(hot, axis=0, keepdims=True)
        return below + count_dot(jnp.broadcast_to(whole, hot.shape), group_earlier), per_chip

    mine_at, mine_in = earlier_chips(mine)
    theirs_at, _ = earlier_chips(theirs)
    far_at, far_in = earlier_chips(far)
    second = core.astype(jnp.float32)
    columns.append(wide_column(theirs, theirs_at, spot_2))
    columns.append(
        wide_column(mine, mine_at + far_at + second * far_in, spot_2)
        + wide_column(far, mine_at + far_at + (1.0 - second) * mine_in, 3 * POOL + far_at)
    )
    return columns


def over_room(number, ring, caps):
    half = ring // 2
    share = forward_share(number, ring, caps[-1])
    worst = jnp.full_like(share, -1.0)
    for k in range(1, half + 1):
        ahead = sum(number[k:half]) + share
        back = sum(number[half + 1 : ring - k + 1]) + number[half] - share
        worst = jnp.maximum(worst, jnp.maximum(ahead, back) - caps[k - 1])
    return worst


def list_room(dest, y_first):
    rows, lanes = dest.shape
    ring_1, caps_1, ring_2, caps_2 = (NY, Y_FIRST, NZ, Z_SECOND) if y_first else (NZ, Z_FIRST, NY, Y_SECOND)
    lane = lax.broadcasted_iota(jnp.int32, (rows, lanes), 1)
    row = lax.broadcasted_iota(jnp.int32, (rows, lanes), 0)
    valid = dest >= 0
    dest_y, dest_z = dest // (NZ * NC), dest // NC % NZ
    dest_1, dest_2 = (dest_y, dest_z) if y_first else (dest_z, dest_y)
    step_1 = (dest_1 - lane // LANES) & (ring_1 - 1)
    step_2 = (dest_2 - row) & (ring_2 - 1)
    left = lax.broadcasted_iota(jnp.int32, (lanes, lanes), 0)
    right = lax.broadcasted_iota(jnp.int32, (lanes, lanes), 1)
    same = jnp.where(left // LANES == right // LANES, 1.0, 0.0)
    tall = jnp.concatenate([jnp.where(valid & (step_1 == k), 1.0, 0.0) for k in range(1, ring_1)], axis=0)
    tall = count_dot(tall, same)
    number = [0.0] + [tall[k * rows : (k + 1) * rows] for k in range(ring_1 - 1)]
    worst = jnp.max(over_room(number, ring_1, caps_1))
    for to in range(ring_1):
        here = valid & (dest_1 == to)
        number = [0.0] + [
            jnp.sum(jnp.where(here & (step_2 == k), 1.0, 0.0), axis=1, keepdims=True) for k in range(1, ring_2)
        ]
        worst = jnp.maximum(worst, jnp.max(over_room(number, ring_2, caps_2)))
    return worst


def plan_kernel(by_y, by_z, picks, room):
    section, core = lax.axis_index("section"), lax.axis_index("core")
    me_y, me_z = lax.axis_index("y"), lax.axis_index("z")
    keys = route_plan(by_y[section, core], by_y[section, 1 - core], False, me_y, me_z, core)
    vals = route_plan(by_z[1 - section, core], by_z[1 - section, 1 - core], True, me_y, me_z, core)
    lane = lax.broadcasted_iota(jnp.int32, (32, 128), 1)
    table = jnp.zeros((32, 128), jnp.float32)
    for base, columns in ((KEYS_COL, keys), (VALS_COL, vals)):
        for at, column in enumerate(columns):
            table = jnp.where(lane == base + at, column, table)
    picks[...] = table.astype(jnp.int32)
    worst = jnp.float32(-1.0)
    for half in range(2):
        for c in range(NC):
            worst = jnp.maximum(worst, list_room(by_y[half, c], False))
            worst = jnp.maximum(worst, list_room(by_z[half, c], True))
    room[0, 0] = worst


def plan_tables(block_dest):
    tables = (block_dest % SHARDS).reshape(2, NY, NZ, NC, BLK_DEV)
    tables = jnp.pad(tables, ((0, 0),) * 4 + ((0, LANES - BLK_DEV),), constant_values=-1)
    by_y = jnp.pad(
        tables.transpose(0, 3, 1, 2, 4).reshape(2, NC, NY, NZ * LANES),
        ((0, 0), (0, 0), (0, 8 - NY), (0, 0)), constant_values=-1,
    )
    by_z = tables.transpose(0, 3, 2, 1, 4).reshape(2, NC, NZ, NY * LANES)
    return by_y, by_z


def plan(block_dest):
    vmem = pl.BlockSpec(memory_space=pltpu.VMEM)
    return pl.pallas_call(
        plan_kernel,
        out_shape=(jax.ShapeDtypeStruct((32, 128), jnp.int32), jax.ShapeDtypeStruct((1, 1), jnp.float32)),
        in_specs=[vmem, vmem],
        out_specs=(vmem, pl.BlockSpec(memory_space=pltpu.SMEM)),
    )(*plan_tables(block_dest))


UNIT = 1024
SLAB = UNIT // NC
TOK_ROWS = 128
PARTS = 2
REQUESTS = 16


RATE = {"x": 0.0475, "y": 0.0475, "z": 0.0475, "core": 0.24, "head": 0.0475}
LATENCY = 1.8
DEPTH = {"x": 1, "y": 1, "z": 2, "core": 4, "head": 1}
FIRST_Z = {"tokens": 0, "keys0": 1, "vals0": 2, "keys1": 3, "vals1": 4}
FIRST_Y = {"tokens": 0, "vals0": 1, "far": 1.5, "keys0": 2, "vals1": 3, "keys1": 4}
UNIT_US = 5.7
SLACK = 3.0


class Transfer:
    def __init__(self, link, megabytes, *moves, small=False):
        self.link, self.megabytes, self.moves, self.small = link, megabytes, moves, small
        self.copies, self.ends, self.left = None, None, megabytes


class Order:
    def __init__(self, send):
        self.send, self.now = send, 0.0
        self.queues = {link: [] for link in RATE}
        self.busy = {link: [] for link in RATE}
        self.seen = dict.fromkeys(RATE, 0.0)

    def advance(self, link):
        while self.busy[link]:
            span = min(t.left for t in self.busy[link]) * len(self.busy[link]) / RATE[link]
            ended = self.seen[link] + span <= self.now
            span = min(span, self.now - self.seen[link])
            part = span * RATE[link] / len(self.busy[link])
            for t in self.busy[link]:
                t.left -= part
            self.seen[link] += span
            if not ended:
                break
            self.busy[link] = [t for t in self.busy[link] if t.left > 1e-9]
        self.seen[link] = self.now

    def foresee(self, link):
        at, gone = self.now, 0.0
        todo = sorted(self.busy[link], key=lambda t: t.left)
        for rank, t in enumerate(todo):
            at += (t.left - gone) * (len(todo) - rank) / RATE[link]
            gone = t.left
            t.ends = at

    def post(self, transfer, rank):
        self.queues[transfer.link].append((rank, transfer))
        self.issue()

    def issue(self):
        for link, queue in self.queues.items():
            self.advance(link)
            while queue and (len(self.busy[link]) < DEPTH[link] or min(queue, key=lambda e: e[0])[1].small):
                entry = min(queue, key=lambda e: e[0])
                queue.remove(entry)
                self.busy[link].append(entry[1])
                entry[1].copies = [self.send(*move) for move in entry[1].moves]
            self.foresee(link)

    def run(self, chains):
        waiting = []

        def step(name, chain):
            for wanted in chain:
                if wanted is None:
                    waiting.append((name, None, chain))
                    return
                if wanted.copies is None and all(wanted is not t for q in self.queues.values() for _, t in q):
                    rank = (FIRST_Y if wanted.link == "y" else FIRST_Z).get(name, 9)
                    self.post(wanted, rank)
                waiting.append((name, wanted, chain))
                return

        for name, chain in chains:
            step(name, chain)
        while waiting:
            self.issue()
            ready = [w for w in waiting if w[1] is not None and w[1].ends is not None]
            compute = [w for w in waiting if w[1] is None]
            first = min(ready, key=lambda w: w[1].ends) if ready else None
            if compute and (first is None or first[1].ends + LATENCY - self.now > SLACK):
                entry = compute[0]
                self.now += UNIT_US
            elif first is not None:
                entry = first
                self.now = max(self.now, first[1].ends + LATENCY)
                for copy in first[1].copies:
                    copy.wait_recv()
            else:
                self.now = min(t.ends for busy in self.busy.values() for t in busy) + 1e-6
                continue
            waiting = [w for w in waiting if w is not entry]
            step(entry[0], entry[2])


def pick(dst, first, count, picks, column, pools):
    def one(j, carry):
        code = picks[j, column]
        block = None
        for at, pool in enumerate(pools):
            row = jnp.clip(code - at * POOL, 0, pool.shape[0] - 1)
            found = pool[row]
            block = found if block is None else jnp.where(code >= at * POOL, found, block)
        dst[first + j] = block
        return carry

    lax.fori_loop(0, count, one, 0)


def move_kernel(picks, queries, kv_own, requests, weight, blocks, mixed, decoded, *scratch):
    kv, w, spread, high, total, accum, att, kept_out, away, got, local_sem, send_sem, recv_sem = scratch[:13]
    buffers = scratch[13:]
    section, core, head = lax.axis_index("section"), lax.axis_index("core"), lax.axis_index("head")
    y, z = lax.axis_index("y"), lax.axis_index("z")
    peers = {
        "x": {"section": 1 - section}, "core": {"core": 1 - core}, "head": {"head": 1 - head},
        "y+": {"y": (y + 1) % NY}, "y-": {"y": (y + NY - 1) % NY},
        "z+": {"z": (z + 1) % NZ}, "z-": {"z": (z + NZ - 1) % NZ},
    }
    count = [0, 0]
    sends = []

    def send(src, dst, to):
        at = count[0]
        count[0] += 1
        copy = pltpu.make_async_remote_copy(
            src_ref=src, dst_ref=dst, send_sem=send_sem.at[at], recv_sem=recv_sem.at[at],
            device_id=peers[to], device_id_type=pl.DeviceIdType.MESH,
        )
        copy.start()
        sends.append(copy)
        return copy

    def sent(copies):
        for copy in copies:
            copy.wait_send()
            sends[:] = [c for c in sends if c is not copy]

    def local(src, dst):
        copy = pltpu.make_async_copy(src, dst, local_sem.at[count[1]])
        count[1] += 1
        copy.start()
        return copy

    part_rows = blocks.shape[2] // PARTS
    slot = part_rows * blocks.shape[3] * 2e-6

    def rows_of(ref, kind, part):
        return ref.at[:, kind, pl.ds(part * part_rows, part_rows)]

    def shard_at(c, yy, zz):
        return (c * NY + yy) * NZ + zz

    own = kv.at[shard_at(core, y, z)]
    parts = [buffers[p * 12 : (p + 1) * 12] for p in range(PARTS)]
    load_kv = local(kv_own, own)
    load_vals = [local(rows_of(blocks, 1, p), parts[p][1]) for p in range(PARTS)]
    load_keys = [local(rows_of(blocks, 0, p), parts[p][0]) for p in range(PARTS)]
    load_weight = local(weight, w)
    barrier = pltpu.get_barrier_semaphore()
    for peer in peers.values():
        pl.semaphore_signal(barrier, inc=1, device_id=peer, device_id_type=pl.DeviceIdType.MESH)
    pl.semaphore_wait(barrier, len(peers))

    def around(stage, arrivals, axis, caps, column, pools):
        cap, back = caps[0], sum(caps)
        ways = ((0, axis + "+", 0), (1, axis + "-", back))
        for at, to, base in ways:
            pick(stage, at * cap, cap, picks, column + at, pools)
        from_stage = Transfer(axis, cap * slot, *[
            (stage.at[pl.ds(at * cap, cap)], arrivals.at[pl.ds(base, cap)], to) for at, to, base in ways
        ])
        yield from_stage
        for k in range(1, len(caps)):
            came, at = sum(caps[: k - 1]), sum(caps[:k])
            yield Transfer(axis, caps[k] * slot, *[
                (arrivals.at[pl.ds(base + came, caps[k])], arrivals.at[pl.ds(base + at, caps[k])], to)
                for _, to, base in ways
            ])
        sent(from_stage.copies)

    def between_cores(stage, arrivals, column, pools):
        pick(stage, 0, BLK_DEV, picks, column, pools)
        crossing = Transfer("core", BLK_DEV * slot, (stage.at[pl.ds(0, BLK_DEV)], arrivals, "core"))
        yield crossing
        sent(crossing.copies)

    outs = []

    def keys_chain(part):
        held, _, _, stage, came_1, came_2, came_3, last = parts[part][:8]
        load_keys[part].wait()
        yield from around(stage, came_1, "z", Z_FIRST, KEYS_COL, [held])
        yield from around(stage, came_2, "y", Y_SECOND, KEYS_COL + 2, [held, came_1])
        yield from between_cores(stage, came_3, KEYS_COL + 4, [held, came_1, came_2])
        pick(stage, 0, BLK_DEV, picks, KEYS_COL + 5, [held, came_1, came_2, came_3])
        yield Transfer("x", BLK_DEV * slot, (stage.at[pl.ds(0, BLK_DEV)], last, "x"))
        outs.append(local(last, rows_of(decoded, 0, part)))

    def vals_chain(part):
        _, inside, held = parts[part][:3]
        stage, came_1, came_2, came_3 = parts[part][8:]
        load_vals[part].wait()
        swap = Transfer("x", BLK_DEV * slot, (inside, held, "x"))
        yield swap
        yield from around(stage, came_1, "y", Y_FIRST, VALS_COL, [held])
        yield from around(stage, came_2, "z", Z_SECOND, VALS_COL + 2, [held, came_1])
        yield from between_cores(stage, came_3, VALS_COL + 4, [held, came_1, came_2])
        sent(swap.copies)
        pick(inside, 0, BLK_DEV, picks, VALS_COL + 5, [held, came_1, came_2, came_3])
        outs.append(local(inside, rows_of(decoded, 1, part)))

    first_query = ((y * NZ + z) * NC + core) * TOK_ROWS
    local_kv, rows, _ = spread.shape
    group = rows // TOK_ROWS

    def row_limits():
        tile_of = requests[pl.ds((y * NZ + z) * NC + core, 1), :]
        starts = jnp.zeros(tile_of.shape, jnp.float32)
        for r in range(1, REQUESTS):
            earlier = jnp.where(requests[...] < r, 1.0, 0.0)
            first = jnp.sum(jnp.sum(earlier, axis=1, keepdims=True), axis=0, keepdims=True)
            starts = jnp.where(tile_of == r, first, starts)
        places = (lax.broadcasted_iota(jnp.int32, tile_of.shape, 1) + first_query).astype(jnp.float32)
        return jnp.concatenate([starts] * group, axis=1), jnp.concatenate([places] * group, axis=1)

    def prepare():
        high[...] = jnp.full_like(high, -1e30)
        total[...] = jnp.zeros_like(total)
        accum[...] = jnp.zeros_like(accum)
        spread[...] = jnp.zeros_like(spread)
        for c in range(local_kv):
            for g in range(group):
                at = (c * group + g) * HD
                spread[c, g * TOK_ROWS : (g + 1) * TOK_ROWS, c * HD : (c + 1) * HD] = queries[
                    :, at : at + HD
                ] * jnp.bfloat16(1.0 / math.sqrt(HD))
        starts, places = row_limits()
        high[4:5, :] = starts
        high[5:6, :] = places

    def slab(half):
        unit, of_core = half // NC, half % NC
        at = shard_at(of_core, 0, 0) + unit * (SLAB // TOK_ROWS)
        block = kv[pl.ds(at, SLAB // TOK_ROWS)].reshape(SLAB, kv.shape[2])
        keys, vals = block[:, : local_kv * HD], block[:, local_kv * HD :].T
        row = lax.broadcasted_iota(jnp.int32, (SLAB, rows), 0)
        pos = unit * UNIT + of_core * TOK_ROWS + (row // TOK_ROWS) * (NC * TOK_ROWS) + row % TOK_ROWS
        pos = pos.astype(jnp.float32)
        keep = (pos >= high[4:5, :]) & (pos <= high[5:6, :])
        for c in range(local_kv):
            scores = lax.dot_general(
                keys, spread[c], (((1,), (1,)), ((), ())), preferred_element_type=jnp.float32
            )
            scores = jnp.where(keep, scores, -1e30)
            before = high[c : c + 1, :]
            now = jnp.maximum(before, jnp.max(scores, axis=0, keepdims=True))
            expo = jnp.exp(scores - now)
            factor = jnp.exp(before - now)
            high[c : c + 1, :] = now
            total[c : c + 1, :] = total[c : c + 1, :] * factor + jnp.sum(expo, axis=0, keepdims=True)
            accum[c] = accum[c] * factor + jnp.dot(
                vals[c * HD : (c + 1) * HD], expo.astype(jnp.bfloat16), preferred_element_type=jnp.float32
            )

    def units(low, top):
        def one(half, carry):
            start = half // NC * UNIT

            @pl.when((start < first_query + TOK_ROWS) & (start + UNIT > first_query - (LONGEST - 1)))
            def _():
                slab(half)

            return carry

        lax.fori_loop(low * NC, top * NC, one, 0)

    def tokens_chain():
        shard = kv_own.shape[0] * kv_own.shape[1] * 2e-6
        load_kv.wait()
        yield Transfer("z", shard, (own, own, "z+"), (own, own, "z-"), small=True)
        for k in range(1, NZ // 2):
            ahead = kv.at[shard_at(core, y, (z - k + NZ) % NZ)]
            back = kv.at[shard_at(core, y, (z + k) % NZ)]
            moves = [(ahead, ahead, "z+")]
            if k < NZ // 2 - 1:
                moves.append((back, back, "z-"))
            yield Transfer("z", shard, *moves, small=True)

        def line(yy):
            return kv.at[pl.ds(shard_at(core, yy, 0), NZ)]

        def some(yy, first):
            return kv.at[pl.ds(shard_at(core, yy, first), NZ // 2)]

        def to_core(yy):
            crossing = Transfer("core", NZ * shard, (line(yy), line(yy), "core"))
            order.post(crossing, 0)
            return crossing

        over, under, across = (y + 1) % NY, (y + NY - 1) % NY, (y + 2) % NY
        around_y = Transfer("y", NZ * shard, (line(y), line(y), "y+"), (line(y), line(y), "y-"))
        order.post(around_y, FIRST_Y["tokens"])
        crossings = [to_core(y)]
        prepare()
        yield around_y
        far = Transfer(
            "y", NZ // 2 * shard,
            (some(under, 0), some(under, 0), "y+"), (some(over, NZ // 2), some(over, NZ // 2), "y-"),
        )
        order.post(far, FIRST_Y["far"])
        crossings += [to_core(under), to_core(over)]
        yield far
        crossings.append(to_core(across))
        for crossing in crossings:
            yield crossing
        for unit in range(kv.shape[0] * TOK_ROWS // UNIT):
            yield None
            units(unit, unit + 1)

        for c in range(local_kv):
            done = (accum[c] / total[c : c + 1, :]).astype(jnp.bfloat16)
            for g in range(group):
                at = (c * group + g) * HD
                att[at : at + HD, :] = done[:, g * TOK_ROWS : (g + 1) * TOK_ROWS]
        load_weight.wait()
        width = w.shape[1] // 2
        attended = att[...].T

        def columns(first):
            first = pl.multiple_of(first, width)
            return jnp.dot(attended, w[:, pl.ds(first, width)], preferred_element_type=jnp.float32)

        away[...] = columns((1 - head) * width).astype(jnp.bfloat16)
        over_heads = Transfer("head", 0.26, (away, got, "head"))
        order.post(over_heads, 0)
        kept_out[...] = columns(head * width)
        yield over_heads
        got[...] = (kept_out[...] + got[...].astype(jnp.float32)).astype(jnp.bfloat16)
        outs.append(local(got, mixed))

    order = Order(send)
    chains = [("tokens", tokens_chain())]
    chains += [("vals%d" % part, vals_chain(part)) for part in range(PARTS)]
    chains += [("keys%d" % part, keys_chain(part)) for part in range(PARTS)]
    order.run(chains)
    for copy in outs:
        copy.wait()
    sent(sends[:])


def move_and_multiply(picks, queries, kv_own, requests, weight, blocks):
    local_kv = kv_own.shape[1] // (2 * HD)
    rows = HEADS // KVH * TOK_ROWS
    part_rows = blocks.shape[2] // PARTS
    half = lambda n: pltpu.VMEM((n, part_rows) + blocks.shape[3:], blocks.dtype)
    vmem, hbm = pl.BlockSpec(memory_space=pltpu.VMEM), pl.BlockSpec(memory_space=pl.ANY)
    width = weight.shape[1] // 2
    copies = 16 + PARTS * 28
    return pl.pallas_call(
        move_kernel,
        out_shape=(
            jax.ShapeDtypeStruct((TOK_ROWS, width), jnp.bfloat16),
            jax.ShapeDtypeStruct(blocks.shape, blocks.dtype),
        ),
        in_specs=[pl.BlockSpec(memory_space=pltpu.SMEM), vmem, hbm, vmem, hbm, hbm],
        out_specs=(hbm, hbm),
        scratch_shapes=[
            pltpu.VMEM((SHARDS,) + kv_own.shape, jnp.bfloat16),
            pltpu.VMEM(weight.shape, jnp.bfloat16),
            pltpu.VMEM((local_kv, rows, local_kv * HD), jnp.bfloat16),
            pltpu.VMEM((8, rows), jnp.float32),
            pltpu.VMEM((8, rows), jnp.float32),
            pltpu.VMEM((local_kv, HD, rows), jnp.float32),
            pltpu.VMEM((weight.shape[0], TOK_ROWS), jnp.bfloat16),
            pltpu.VMEM((TOK_ROWS, width), jnp.float32),
            pltpu.VMEM((TOK_ROWS, width), jnp.bfloat16),
            pltpu.VMEM((TOK_ROWS, width), jnp.bfloat16),
            pltpu.SemaphoreType.DMA((3 + 4 * PARTS,)),
            pltpu.SemaphoreType.DMA((copies,)),
            pltpu.SemaphoreType.DMA((copies,)),
        ]
        + [
            half(n)
            for _ in range(PARTS)
            for n in (
                BLK_DEV, BLK_DEV, BLK_DEV,
                2 * max(Z_FIRST[0], Y_SECOND[0]), 2 * sum(Z_FIRST), 2 * sum(Y_SECOND), BLK_DEV, BLK_DEV,
                2 * max(Y_FIRST[0], Z_SECOND[0]), 2 * sum(Y_FIRST), 2 * sum(Z_SECOND), BLK_DEV,
            )
        ],
        compiler_params=pltpu.CompilerParams(
            collective_id=0, has_side_effects=True, vmem_limit_bytes=63 * 1024 * 1024
        ),
        cost_estimate=pl.CostEstimate(flops=10**10, bytes_accessed=20 * 2**20, transcendentals=10**7),
    )(picks, queries, kv_own, requests, weight, blocks)


def per_device(queries, keyvals, span_req, prefill_blocks, block_dest, out_weight):
    picks, room = plan(block_dest)
    kv_own = keyvals[0].reshape(TOK_ROWS, -1)
    requests = span_req.reshape(SHARDS, TOK_ROWS)
    mixed, routed = move_and_multiply(picks, queries[0], kv_own, requests, out_weight, prefill_blocks)
    decode_blocks = lax.cond(
        room[0, 0] <= 0.0,
        lambda done, blocks, dest: done,
        lambda done, blocks, dest: hand_over_padded(blocks, dest),
        routed, prefill_blocks, block_dest,
    )
    return mixed[None], decode_blocks


def solution(mesh):
    fine = Mesh(mesh.devices.reshape(2, NY, NZ, NC, 2), ("section",) + TOK + ("head",))
    return jax.shard_map(
        per_device,
        mesh=fine,
        in_specs=(
            P("section", TOK, "head"),
            P("section", TOK, None, "head"),
            P("section", None),
            P(("section",) + TOK, None, None, "head"),
            P(),
            P("head", None),
        ),
        out_specs=(P("section", TOK, "head"), P(("section",) + TOK, None, None, "head")),
        check_vma=False,
    )
```
